32 devices in a mesh: hist: 8 (over z, y), col: 4 (over x, core).
Axes of the slice: x: 2, y: 2, z: 4, core: 2. Of those that a mesh axis runs over, the one named last changes fastest.
Arguments:
- sigma_ret: bfloat16 [4, 32, 64, 128], P(None, 'hist', 'col'), may hold values from -6 to 6
- sigma_less: bfloat16 [4, 32, 64, 128], P(None, 'hist', 'col'), may hold values from -6 to 6
- green_less: bfloat16 [32, 96, 64, 128], P('hist', 'col'), may hold values from -0.09375 to 0.09375
- green_adv: bfloat16 [32, 96, 64, 128], P('hist', 'col'), may hold values from -0.09375 to 0.09375
- time_now: int32 [4], replicated, may hold values from 16 to 31, as said below
- col_start: int32 [96], P('col'), may hold values from 0 to 15
Outputs:
- collision: bfloat16 [4, 96, 64, 128], P(None, 'col')
The draws below stay inside these ranges and needn't reach their ends.
Inputs may be any that keep to these rules, and one draw needn't show every extreme that they name: Some time row has time_now = 31.
All inputs are finite; a program needn't handle non-finite values.
Results may differ from the reference program's by a relative error of at most 0.001.
Values may be sent and summed in bfloat16 or wider, within the bound.
No kernel may reach another device: no remote copies, remote signals or barrier semaphores. Data moves between devices by JAX's collectives and lax.ppermute only.
A program may use at most 64 MiB of HBM per device.

```python
import jax
import jax.numpy as jnp
from jax import lax

NORB = 64
NT = 4
TB = 32
TC = 96


def draw_time_now(key, part):
    key = jax.random.fold_in(key, 7)
    key_vals = jax.random.fold_in(key, 1)
    key_pick = jax.random.fold_in(key, 2)
    values = jax.random.randint(key_vals, (NT,), TB // 2, TB, dtype=jnp.int32)
    picked = jax.random.randint(key_pick, (), 0, NT, dtype=jnp.int32)
    rows = jnp.arange(NT, dtype=jnp.int32)
    return jnp.where(rows == picked, jnp.int32(TB - 1), values).astype(jnp.int32)


def touch_ends(drawn, stream_key, low, high):
    longest = drawn.shape.index(max(drawn.shape))
    spots = []
    for shift in (0, 1):
        where = [jax.random.randint(jax.random.fold_in(stream_key, axis), (), 0, length) for axis, length in enumerate(drawn.shape)]
        where[longest] = (where[longest] + shift) % drawn.shape[longest]
        spots.append(tuple(where))
    return drawn.at[spots[0]].set(low).at[spots[1]].set(high)


def level_of(rng, shape, cuts, least, largest):
    gain, own = 1.0, jax.random.fold_in(rng, 6)
    for axis_at, blocks in cuts:
        steps = jnp.exp(jax.random.uniform(jax.random.fold_in(own, axis_at), (blocks,), jnp.float32, least / len(cuts), largest / len(cuts)))
        gain = gain * jnp.repeat(steps, shape[axis_at] // blocks).reshape([-1 if axis == axis_at else 1 for axis in range(len(shape))])
    return gain


def centred(rng, extent, spread, most, pieces=(), kind=jnp.bfloat16):
    result = jax.random.normal(rng, extent, jnp.float32) * spread
    if len(pieces) > 0:
        result = level_of(rng, extent, pieces, -0.22, 0.18) * result
    return jnp.clip(result, min=-most, max=most).astype(kind)


def setup_inputs(seed: int = 0) -> dict:
    arg_keys = jax.random.split(jax.random.key(seed), 7)
    return {
        "sigma_ret": centred(arg_keys[0], (NT, TB, NORB, 2 * NORB), 1.0, 6.0, ((1, 8), (2, 4))),
        "sigma_less": centred(arg_keys[1], (NT, TB, NORB, 2 * NORB), 1.0, 6.0, ((1, 8), (2, 4))),
        "green_less": centred(arg_keys[2], (TB, TC, NORB, 2 * NORB), (2 * TB * NORB) ** -0.5, 0.09375, ((0, 8), (1, 4))),
        "green_adv": centred(arg_keys[3], (TB, TC, NORB, 2 * NORB), (2 * TB * NORB) ** -0.5, 0.09375, ((0, 8), (1, 4))),
        "time_now": draw_time_now(jax.random.fold_in(arg_keys[6], 71), 0),
        "col_start": touch_ends(jax.random.randint(arg_keys[5], (TC,), 0, TB // 2), jax.random.fold_in(arg_keys[5], 1), 0, (TB // 2) - 1).astype(jnp.int32),
    }


def widen(green):
    real_part = green[..., :NORB]
    imag_part = green[..., NORB:]
    lower = jnp.concatenate([-imag_part, real_part], axis=-1)
    return jnp.concatenate([green, lower], axis=-2)


def reference(sigma_ret, sigma_less, green_less, green_adv, time_now, col_start):
    tbar = jnp.arange(TB, dtype=jnp.int32)
    before = (tbar[None, :] <= time_now[:, None])[:, :, None, None]
    left_r = jnp.where(before, sigma_ret.astype(jnp.float32), 0.0)
    left_l = jnp.where(before, sigma_less.astype(jnp.float32), 0.0)

    def one_column(column):
        g_less, g_adv, start = column
        after = (tbar >= start)[:, None, None]
        b_less = jnp.where(after, widen(g_less.astype(jnp.float32)), 0.0)
        b_adv = jnp.where(after, widen(g_adv.astype(jnp.float32)), 0.0)
        first = jnp.einsum("tbik,bkn->tin", left_r, b_less, precision=lax.Precision.HIGHEST)
        second = jnp.einsum("tbik,bkn->tin", left_l, b_adv, precision=lax.Precision.HIGHEST)
        return first + second

    cols = lax.map(one_column, (jnp.swapaxes(green_less, 0, 1), jnp.swapaxes(green_adv, 0, 1), col_start))
    return jnp.swapaxes(cols, 0, 1).astype(jnp.bfloat16)
```

```python
import functools

import jax
import jax.numpy as jnp
from jax import lax
from jax.experimental import pallas as pl
from jax.experimental.pallas import tpu as pltpu
from jax.sharding import PartitionSpec as P

BITS = {"y": 0, "z0": 1, "z1": 2}
ORDERS = ((("y", "z0", "z1", "z0", "y"), ("z0", "y", "z1", "z0", "y")), (("y", "z1", "z0", "y", "z1"), ("z1", "y", "z0", "z1", "y")), (("y", "z0", "z1", "y", "z0"), ("z0", "y", "z1", "z0", "y")), (("z1", "y", "z0", "z1", "y"), ("y", "z0", "z1", "y", "z0")))
STEPS = (0, 1, 2, 0, 3, 1, 2, 0, 3, 1, 2, 0, 3, 2, 1, 3)
PLACES = (((0, 0), (1, 0), (2, 0), (3, 0), (0, 1)), ((2, 1), (1, 1), (3, 1)))
CHAIN = (1, 1, 1, 1, 1, 1, 1, 1, 1, 1, 1, 1, 1, 1, 1, 1)
FIRST, COL, CORE, FIELDS = 4, 5, 6, 8
GROUP = 3
STEPS_PER_OCTAVE = 128.0
TOP = 32512.0
LEAST = 2.0 ** -110
MIB = 2 ** 20
PARAMS = pltpu.CompilerParams(vmem_limit_bytes=40 * MIB)


def widen(green, norb):
    real_part = green[..., :norb]
    imag_part = green[..., norb:]
    lower = jnp.concatenate([-imag_part, real_part], axis=-1)
    return jnp.concatenate([green, lower], axis=-2)


def encode(read, tiles, ni, out_ref):
    rows = []
    for first in range(0, tiles, GROUP):
        values = read(first)
        most = jnp.max(jnp.max(jnp.abs(values), axis=0), axis=0, keepdims=True)
        index = jnp.ceil(jnp.log2(jnp.maximum(most, LEAST) * (1.0 / TOP)) * STEPS_PER_OCTAVE)
        codes = jnp.round(values * jnp.exp2(index * (-1.0 / STEPS_PER_OCTAVE))[None])
        out_ref[first:first + GROUP] = codes.astype(jnp.int32).astype(jnp.int16)
        rows.append(index)
    rows = rows + [jnp.zeros_like(rows[0])] * (ni - len(rows))
    out_ref[tiles] = jnp.concatenate(rows, axis=0).astype(jnp.int32).astype(jnp.int16)


def decode(in_ref, tiles):
    index = in_ref[tiles].astype(jnp.int32).astype(jnp.float32)
    scales = jnp.exp2(index * (1.0 / STEPS_PER_OCTAVE))
    return [
        in_ref[first:first + GROUP].astype(jnp.int32).astype(jnp.float32) * scales[g:g + 1][None]
        for g, first in enumerate(range(0, tiles, GROUP))
    ]


def pack_left(info, at, sigma_ref, left_ref, row):
    _, nt, nb, ni, width = sigma_ref.shape
    half = width // 2
    for t in range(nt):
        for b in range(nb):
            live = info[FIRST] + b <= info[at + t]
            ret = jnp.where(live, sigma_ref[0, t, b], jnp.zeros((), jnp.bfloat16))
            less = jnp.where(live, sigma_ref[1, t, b], jnp.zeros((), jnp.bfloat16))
            cols = slice(b * width, (b + 1) * width)
            rows = slice(row + t * ni, row + (t + 1) * ni)
            left_ref[rows, cols] = jnp.concatenate([ret[:, :half], less[:, :half]], axis=1)
            rows = slice(row + (nt + t) * ni, row + (nt + t + 1) * ni)
            left_ref[rows, cols] = jnp.concatenate([ret[:, half:], less[:, half:]], axis=1)


def relative(info, orders, bits):
    spots = [[lax.bitwise_xor(info[BITS[d]], bits[d]) for d in order] for order in orders]
    return [jnp.where(info[CORE] == 0, *pair) for pair in zip(*spots)]


def spots_of(info, orders, nt):
    dims = [order[:3] for order in orders]
    return [[relative(info, dims, {"y": side, "z0": t % 2, "z1": t // 2}) for t in range(nt)] for side in range(2)]


def add_pair(spots, both, pair, term_ref):
    ni, width = term_ref.shape[-2:]
    half_columns = term_ref.shape[3]
    rows = both.shape[0] // 2
    lane = lax.broadcasted_iota(jnp.int32, (rows, width), 1)
    for at in range(2):
        cut = both[:, at * width:(at + 1) * width]
        turned = pltpu.roll(cut[rows:], width // 2, 1)
        value = cut[:rows] + jnp.where(lane < width // 2, -turned, turned)
        side, c = divmod(2 * pair + at, half_columns)
        for t in range(rows // ni):
            term_ref[tuple(spots[side][t]) + (c,)] = value[t * ni:(t + 1) * ni]


def part_kernel(orders, info, *refs):
    n = len(orders)
    sigma_refs, (gless_ref, gadv_ref) = refs[:n], refs[n:n + 2]
    outs, (left_ref, term_ref) = refs[-2 * n - 2:-2], refs[-2:]
    nb, ncol, norb, width = gless_ref.shape
    rows = left_ref.shape[0] // n
    for at, sigma_ref in enumerate(sigma_refs):
        pack_left(info, FIELDS, sigma_ref, left_ref, at * rows)
    spots = [spots_of(info, order, rows // (2 * term_ref.shape[-2])) for order in orders]
    for pair in range(ncol // 2):
        sides = []
        for c in (2 * pair, 2 * pair + 1):
            parts = []
            for b in range(nb):
                parts += [gless_ref[b, c], gadv_ref[b, c]]
            sides.append(jnp.concatenate(parts, axis=0))
        both = jnp.dot(left_ref[...], jnp.concatenate(sides, axis=1), preferred_element_type=jnp.float32)
        for at in range(n):
            add_pair(spots[at], both[at * rows:(at + 1) * rows], pair, term_ref.at[at])
    for at in range(n):
        keep_ref, out_ref = outs[2 * at:2 * at + 2]
        _, n1, n2, half_columns, ni, _ = term_ref.shape[1:]
        keep_ref[0] = term_ref[at, 0]

        def read(first):
            block, c = divmod(first, half_columns)
            a, b = divmod(block, n2)
            return term_ref[at, 1, a, b, c:c + GROUP]

        encode(read, n1 * n2 * half_columns, ni, out_ref)


def fold_kernel(sum_ref, in_ref, *refs):
    keep_ref, out_ref, term_ref = refs[-3:]
    _, nd, nc, ni, width = keep_ref.shape
    tiles = nd * nc
    came = decode(in_ref, 2 * tiles)
    for g, first in enumerate(range(0, tiles, GROUP)):
        d, c = divmod(first, nc)
        keep_ref[0, d, c:c + GROUP] = sum_ref[0, 0, d, c:c + GROUP] + came[g]
        term_ref[first:first + GROUP] = sum_ref[0, 1, d, c:c + GROUP] + came[g + tiles // GROUP]
    encode(lambda first: term_ref[first:first + GROUP], tiles, ni, out_ref)


def cross_kernel(sum_ref, in_ref, *refs):
    out_ref, term_ref = refs[-2:]
    _, nd, nc, ni, width = sum_ref.shape
    for g, came in enumerate(decode(in_ref, nd * nc)):
        d, c = divmod(g * GROUP, nc)
        term_ref[g * GROUP:(g + 1) * GROUP] = sum_ref[0, d, c:c + GROUP] + came
    encode(lambda first: term_ref[first:first + GROUP], nd * nc, ni, out_ref)


def final_kernel(mine_ref, other_ref, *refs):
    out_ref = refs[-1]
    nd, nc, ni, width = out_ref.shape
    mine, other = decode(mine_ref, nd * nc), decode(other_ref, nd * nc)
    half = len(mine) // 2
    for g in range(len(mine)):
        d, c = divmod(g * GROUP, nc)
        out_ref[d, c:c + GROUP] = (mine[g] + other[(g + half) % len(mine)]).astype(jnp.bfloat16)


def merge_kernel(mine_ref, other_ref, *refs):
    out_ref = refs[-1]
    out_ref[0] = mine_ref[...]
    out_ref[1] = other_ref[...]


def copy_kernel(in_ref, *refs):
    refs[-1][...] = in_ref[...]


def place_kernel(items, info, *refs):
    blocks, out_ref, sem = refs[:len(items)], refs[-2], refs[-1]
    copies = []
    for block, (chunk, orders, last) in zip(blocks, items):
        nc, ni, _ = block.shape[-3:]
        row = pl.multiple_of(lax.bitwise_xor(info[COL], chunk) * ni, ni)
        for second in range(2):
            for first in range(2):
                places = []
                for order in orders:
                    bits = dict(zip(order[2:], (first, second, last)))
                    places.append([lax.bitwise_xor(info[BITS[d]], bits[d]) for d in ("y", "z0", "z1")])
                y, z0, z1 = (jnp.where(info[CORE] == 0, *pair) for pair in zip(*places))
                target = out_ref.at[2 * z1 + z0, pl.ds(y * nc, nc), pl.ds(row, ni)]
                copies.append(pltpu.make_async_copy(block.at[second, first], target, sem.at[len(copies)]))
    for copy in copies:
        copy.start()
    for copy in copies:
        copy.wait()


def staged(sigma_ret, sigma_less, green_less, green_adv, time_now, col_start, n_hist, n_col):
    nt, nb, ni, width = sigma_ret.shape
    _, ncol, norb, _ = green_less.shape
    nc = ncol // 2
    hist = lax.axis_index("hist")
    col = lax.axis_index("col")
    field = jnp.arange(FIELDS, dtype=jnp.int32)
    bit = lax.shift_right_logical(jnp.where(field == CORE, col << CORE, hist), field) & 1
    own = jnp.where(field == FIRST, hist * nb, jnp.where(field == COL, col, bit))
    info = jnp.concatenate([own, time_now])

    def swap(v, chunk, stage):
        pairs = []
        for h in range(n_hist):
            for c in range(n_col):
                partner = h ^ (1 << BITS[ORDERS[chunk][c % 2][stage]])
                pairs.append((h * n_col + c, partner * n_col + c))
        return lax.ppermute(v, ("hist", "col"), pairs)

    def swap_col(v, k):
        return lax.ppermute(v, "col", [(i, i ^ k) for i in range(n_col)])

    smem = pl.BlockSpec(memory_space=pltpu.SMEM)
    vmem = pl.BlockSpec(memory_space=pltpu.VMEM)
    hbm = pl.BlockSpec(memory_space=pltpu.HBM)

    def codes_of(n):
        return jax.ShapeDtypeStruct((n * nc + 1, ni, width), jnp.int16)

    own_sigma = jnp.stack([sigma_ret, sigma_less])
    tbar = hist * nb + jnp.arange(nb, dtype=jnp.int32)
    after = (tbar[:, None] >= col_start[None, :])[:, :, None, None]
    zero = jnp.zeros((), green_less.dtype)
    masked = [jnp.where(after, green, zero) for green in (green_less, green_adv)]
    near = swap_col(own_sigma, 1)
    far = swap_col(own_sigma, 2)

    def call(kernel, out_shape, args, before, scratch=(), cost=None, specs=()):
        args = list(args) + ([] if before is None else [before])
        many = isinstance(out_shape, list)
        return pl.pallas_call(
            kernel,
            out_shape=out_shape,
            in_specs=list(specs) + [vmem] * (len(args) - len(specs)),
            out_specs=[vmem] * len(out_shape) if many else vmem,
            scratch_shapes=list(scratch),
            compiler_params=PARAMS,
            cost_estimate=cost,
            name=kernel.func.__name__ if isinstance(kernel, functools.partial) else kernel.__name__,
        )(*args)

    def partial(orders, blocks, before):
        n = len(orders)
        rows = 2 * nt * ni
        keep = jax.ShapeDtypeStruct((1, 2, 2, nc, ni, width), jnp.float32)
        flops = 2 * n * rows * 2 * nb * norb * ncol * width
        out = call(
            functools.partial(part_kernel, orders),
            [keep, codes_of(4)] * n,
            [info, *blocks, *masked],
            before,
            [pltpu.VMEM((n * rows, nb * width), jnp.bfloat16),
             pltpu.VMEM((n, 2, 2, 2, nc, ni, width), jnp.float32)],
            pl.CostEstimate(flops=flops, bytes_accessed=green_less.size * 4, transcendentals=0),
            [smem],
        )
        return [out[2 * at:2 * at + 2] for at in range(n)]

    def terms(n):
        return [pltpu.VMEM((n * nc, ni, width), jnp.float32)]

    def fold(state, chunk, before):
        sums, codes = state
        keep = jax.ShapeDtypeStruct((1, 2, nc, ni, width), jnp.float32)
        state = call(fold_kernel, [keep, codes_of(2)], [sums, swap(codes, chunk, 0)], before, terms(2))
        return state, state[1]

    def cross(state, chunk, before):
        sums, codes = state
        codes = call(cross_kernel, codes_of(2), [sums, swap(codes, chunk, 1)], before, terms(2))
        return codes, codes

    def final(codes, chunk, before):
        out = jax.ShapeDtypeStruct((2, nc, ni, width), jnp.bfloat16)
        out = call(final_kernel, out, [codes, swap(codes, chunk, 2)], before)
        return out, out

    def merge(mine, chunk, before):
        out = jax.ShapeDtypeStruct((2,) + mine.shape, mine.dtype)
        out = call(merge_kernel, out, [mine, swap(mine, chunk, 3)], before)
        return out, out

    def put(items, out):
        extra = [] if out is None else [out]
        n = len(items)
        return pl.pallas_call(
            functools.partial(place_kernel, [(k, ORDERS[k], last) for k, last in items]),
            out_shape=jax.ShapeDtypeStruct((nt, ncol, norb, width), jnp.bfloat16),
            in_specs=[smem] + [vmem] * n + [hbm] * len(extra),
            out_specs=hbm,
            scratch_shapes=[pltpu.SemaphoreType.DMA((4 * n,))],
            input_output_aliases={1 + n: 0} if extra else {},
            compiler_params=PARAMS,
            name="place_part",
        )(info, *[blocks[k][last] for k, last in items], *extra)

    state = partial(ORDERS[:2], [own_sigma, near], None)
    passed = call(copy_kernel, jax.ShapeDtypeStruct(far.shape, far.dtype), [far], state[1][1])
    state += partial(ORDERS[2:3], [far], passed)
    state += partial(ORDERS[3:], [swap_col(passed, 1)], state[2][1])
    last = state[3][1]
    todo = [[fold, cross, final, merge] for _ in range(n_col)]
    for k, chained in zip(STEPS, CHAIN):
        state[k], last = todo[k].pop(0)(state[k], k, last if chained else None)
    blocks = [(state[k], swap(state[k], k, 4)) for k in range(n_col)]
    out = None
    for items in PLACES:
        out = put(items, out)
    return out


def plain(sigma_ret, sigma_less, green_less, green_adv, time_now, col_start):
    norb = green_less.shape[2]
    tb_local = green_less.shape[0]
    full_ret = lax.all_gather(sigma_ret, "col", axis=2, tiled=True)
    full_less = lax.all_gather(sigma_less, "col", axis=2, tiled=True)
    tbar = lax.axis_index("hist") * tb_local + jnp.arange(tb_local, dtype=jnp.int32)
    zero = jnp.zeros((), green_less.dtype)
    before = (tbar[None, :] <= time_now[:, None])[:, :, None, None]
    full_ret = jnp.where(before, full_ret, zero)
    full_less = jnp.where(before, full_less, zero)
    after = (tbar[:, None] >= col_start[None, :])[:, :, None, None]
    b_less = jnp.where(after, widen(green_less, norb), zero)
    b_adv = jnp.where(after, widen(green_adv, norb), zero)
    term = jnp.einsum("tbik,bckn->tcin", full_ret, b_less, preferred_element_type=jnp.float32)
    term = term + jnp.einsum("tbik,bckn->tcin", full_less, b_adv, preferred_element_type=jnp.float32)
    return lax.psum(term, "hist").astype(jnp.bfloat16)


def solution(mesh):
    n_hist, n_col = mesh.shape["hist"], mesh.shape["col"]

    def on_device(*args):
        nt, ncol = args[0].shape[0], args[2].shape[1]
        if n_hist == 8 and nt == 4 and n_col == 4 and ncol % 4 == 0 and ncol % (2 * GROUP) == 0:
            return staged(*args, n_hist, n_col)
        return plain(*args)

    return jax.shard_map(
        on_device,
        mesh=mesh,
        in_specs=(
            P(None, "hist", "col", None),
            P(None, "hist", "col", None),
            P("hist", "col", None, None),
            P("hist", "col", None, None),
            P(),
            P("col"),
        ),
        out_specs=P(None, "col", None, None),
        check_vma=False,
    )
```

```python
import functools

import jax
import jax.numpy as jnp
from jax import lax
from jax.experimental import pallas as pl
from jax.experimental.pallas import tpu as pltpu
from jax.sharding import PartitionSpec as P

BITS = {"y": 0, "z0": 1, "z1": 2}
ORDERS = ((("y", "z0", "z1", "y", "z0"), ("y", "z0", "z1", "y", "z0")), (("z1", "y", "z0", "z1", "y"), ("z1", "y", "z0", "z1", "y")), (("y", "z0", "z1", "z0", "y"), ("y", "z0", "z1", "z0", "y")), (("y", "z0", "z1", "y", "z0"), ("y", "z0", "z1", "y", "z0")))
STEPS = (0, 2, 0, 1, 3, 2, 1, 0, 3, 2, 1, 0, 3, 2, 1, 3)
PLACES = (((0, 0), (1, 0), (2, 0), (3, 0), (0, 1)), ((1, 1), (2, 1), (3, 1)))
GROUP = 3
STEPS_PER_OCTAVE = 128.0
TOP = 32512.0
LEAST = 2.0 ** -110
MIB = 2 ** 20
PARAMS = pltpu.CompilerParams(vmem_limit_bytes=40 * MIB)


def widen(green, norb):
    real_part = green[..., :norb]
    imag_part = green[..., norb:]
    lower = jnp.concatenate([-imag_part, real_part], axis=-1)
    return jnp.concatenate([green, lower], axis=-2)


def encode(read, tiles, ni, out_ref):
    rows = []
    for first in range(0, tiles, GROUP):
        values = read(first)
        most = jnp.max(jnp.max(jnp.abs(values), axis=0), axis=0, keepdims=True)
        index = jnp.ceil(jnp.log2(jnp.maximum(most, LEAST) * (1.0 / TOP)) * STEPS_PER_OCTAVE)
        codes = jnp.round(values * jnp.exp2(index * (-1.0 / STEPS_PER_OCTAVE))[None])
        out_ref[first:first + GROUP] = codes.astype(jnp.int32).astype(jnp.int16)
        rows.append(index)
    rows = rows + [jnp.zeros_like(rows[0])] * (ni - len(rows))
    out_ref[tiles] = jnp.concatenate(rows, axis=0).astype(jnp.int32).astype(jnp.int16)


def decode(in_ref, tiles):
    index = in_ref[tiles].astype(jnp.int32).astype(jnp.float32)
    scales = jnp.exp2(index * (1.0 / STEPS_PER_OCTAVE))
    return [
        in_ref[first:first + GROUP].astype(jnp.int32).astype(jnp.float32) * scales[g:g + 1][None]
        for g, first in enumerate(range(0, tiles, GROUP))
    ]


def pack_left(sigma_ref, keep_ref, left_ref, row):
    _, nt, nb, ni, width = sigma_ref.shape
    half = width // 2
    for t in range(nt):
        for b in range(nb):
            ret = sigma_ref[0, t, b] * keep_ref[t, b]
            less = sigma_ref[1, t, b] * keep_ref[t, b]
            cols = slice(b * width, (b + 1) * width)
            rows = slice(row + t * ni, row + (t + 1) * ni)
            left_ref[rows, cols] = jnp.concatenate([ret[:, :half], less[:, :half]], axis=1)
            rows = slice(row + (nt + t) * ni, row + (nt + t + 1) * ni)
            left_ref[rows, cols] = jnp.concatenate([ret[:, half:], less[:, half:]], axis=1)


def own_bits():
    hist = lax.axis_index("hist")
    bits = {d: lax.shift_right_logical(hist, at) & 1 for d, at in BITS.items()}
    return bits, lax.axis_index("col") & 1


def relative(own, core, orders, bits):
    spots = [[lax.bitwise_xor(own[d], bits[d]) for d in order] for order in orders]
    return [one if one is two else jnp.where(core == 0, one, two) for one, two in zip(*spots)]


def spots_of(orders, nt):
    own, core = own_bits()
    dims = [order[:3] for order in orders]
    return [[relative(own, core, dims, {"y": side, "z0": t % 2, "z1": t // 2}) for t in range(nt)] for side in range(2)]


def add_pair(spots, both, pair, term_ref):
    ni, width = term_ref.shape[-2:]
    half_columns = term_ref.shape[3]
    rows = both.shape[0] // 2
    lane = lax.broadcasted_iota(jnp.int32, (rows, width), 1)
    for at in range(2):
        cut = both[:, at * width:(at + 1) * width]
        turned = pltpu.roll(cut[rows:], width // 2, 1)
        value = cut[:rows] + jnp.where(lane < width // 2, -turned, turned)
        side, c = divmod(2 * pair + at, half_columns)
        for t in range(rows // ni):
            term_ref[tuple(spots[side][t]) + (c,)] = value[t * ni:(t + 1) * ni]


def part_kernel(orders, keep_ref, *refs):
    n = len(orders)
    sigma_refs, (gless_ref, gadv_ref) = refs[:n], refs[n:n + 2]
    outs, (left_ref, term_ref) = refs[-2 * n - 2:-2], refs[-2:]
    nb, ncol, norb, width = gless_ref.shape
    rows = left_ref.shape[0] // n
    for at, sigma_ref in enumerate(sigma_refs):
        pack_left(sigma_ref, keep_ref, left_ref, at * rows)
    spots = [spots_of(order, rows // (2 * term_ref.shape[-2])) for order in orders]
    for pair in range(ncol // 2):
        sides = []
        for c in (2 * pair, 2 * pair + 1):
            parts = []
            for b in range(nb):
                parts += [gless_ref[b, c], gadv_ref[b, c]]
            sides.append(jnp.concatenate(parts, axis=0))
        both = jnp.dot(left_ref[...], jnp.concatenate(sides, axis=1), preferred_element_type=jnp.float32)
        for at in range(n):
            add_pair(spots[at], both[at * rows:(at + 1) * rows], pair, term_ref.at[at])
    for at in range(n):
        kept_ref, out_ref = outs[2 * at:2 * at + 2]
        _, n1, n2, half_columns, ni, _ = term_ref.shape[1:]
        kept_ref[0] = term_ref[at, 0]

        def read(first):
            block, c = divmod(first, half_columns)
            a, b = divmod(block, n2)
            return term_ref[at, 1, a, b, c:c + GROUP]

        encode(read, n1 * n2 * half_columns, ni, out_ref)


def fold_kernel(sum_ref, in_ref, *refs):
    keep_ref, out_ref, term_ref = refs[-3:]
    _, nd, nc, ni, width = keep_ref.shape
    tiles = nd * nc
    came = decode(in_ref, 2 * tiles)
    for g, first in enumerate(range(0, tiles, GROUP)):
        d, c = divmod(first, nc)
        keep_ref[0, d, c:c + GROUP] = sum_ref[0, 0, d, c:c + GROUP] + came[g]
        term_ref[first:first + GROUP] = sum_ref[0, 1, d, c:c + GROUP] + came[g + tiles // GROUP]
    encode(lambda first: term_ref[first:first + GROUP], tiles, ni, out_ref)


def cross_kernel(sum_ref, in_ref, *refs):
    out_ref, term_ref = refs[-2:]
    _, nd, nc, ni, width = sum_ref.shape
    for g, came in enumerate(decode(in_ref, nd * nc)):
        d, c = divmod(g * GROUP, nc)
        term_ref[g * GROUP:(g + 1) * GROUP] = sum_ref[0, d, c:c + GROUP] + came
    encode(lambda first: term_ref[first:first + GROUP], nd * nc, ni, out_ref)


def final_kernel(mine_ref, other_ref, *refs):
    out_ref = refs[-1]
    nd, nc, ni, width = out_ref.shape
    mine, other = decode(mine_ref, nd * nc), decode(other_ref, nd * nc)
    half = len(mine) // 2
    for g in range(len(mine)):
        d, c = divmod(g * GROUP, nc)
        out_ref[d, c:c + GROUP] = (mine[g] + other[(g + half) % len(mine)]).astype(jnp.bfloat16)


def merge_kernel(mine_ref, other_ref, *refs):
    out_ref = refs[-1]
    out_ref[0] = mine_ref[...]
    out_ref[1] = other_ref[...]


def copy_kernel(in_ref, *refs):
    refs[-1][...] = in_ref[...]


def place_kernel(items, *refs):
    blocks, out_ref, sem = refs[:len(items)], refs[-2], refs[-1]
    own, core = own_bits()
    copies = []
    for block, (chunk, orders, last) in zip(blocks, items):
        nc, ni, _ = block.shape[-3:]
        row = pl.multiple_of(lax.bitwise_xor(lax.axis_index("col"), chunk) * ni, ni)
        for second in range(2):
            for first in range(2):
                places = []
                for order in orders:
                    bits = dict(zip(order[2:], (first, second, last)))
                    places.append([lax.bitwise_xor(own[d], bits[d]) for d in ("y", "z0", "z1")])
                y, z0, z1 = (jnp.where(core == 0, *pair) for pair in zip(*places))
                target = out_ref.at[2 * z1 + z0, pl.ds(y * nc, nc), pl.ds(row, ni)]
                copies.append(pltpu.make_async_copy(block.at[second, first], target, sem.at[len(copies)]))
    for copy in copies:
        copy.start()
    for copy in copies:
        copy.wait()


def staged(sigma_ret, sigma_less, green_less, green_adv, time_now, col_start, n_hist, n_col):
    nt, nb, ni, width = sigma_ret.shape
    _, ncol, norb, _ = green_less.shape
    nc = ncol // 2
    hist = lax.axis_index("hist")
    def swap(v, chunk, stage):
        pairs = []
        for h in range(n_hist):
            for c in range(n_col):
                partner = h ^ (1 << BITS[ORDERS[chunk][c % 2][stage]])
                pairs.append((h * n_col + c, partner * n_col + c))
        return lax.ppermute(v, ("hist", "col"), pairs)

    def swap_col(v, k):
        return lax.ppermute(v, "col", [(i, i ^ k) for i in range(n_col)])

    vmem = pl.BlockSpec(memory_space=pltpu.VMEM)
    hbm = pl.BlockSpec(memory_space=pltpu.HBM)

    def codes_of(n):
        return jax.ShapeDtypeStruct((n * nc + 1, ni, width), jnp.int16)

    own_sigma = jnp.stack([sigma_ret, sigma_less])
    tbar = hist * nb + jnp.arange(nb, dtype=jnp.int32)
    after = (tbar[:, None] >= col_start[None, :])[:, :, None, None]
    zero = jnp.zeros((), green_less.dtype)
    before = (tbar[None, :] <= time_now[:, None]).astype(sigma_ret.dtype)
    keep = jnp.broadcast_to(before[:, :, None, None], sigma_ret.shape)
    masked = [jnp.where(after, green, zero) for green in (green_less, green_adv)]
    near = swap_col(own_sigma, 1)
    far = swap_col(own_sigma, 2)

    def call(kernel, out_shape, args, before, scratch=(), cost=None):
        args = list(args) + ([] if before is None else [before])
        many = isinstance(out_shape, list)
        return pl.pallas_call(
            kernel,
            out_shape=out_shape,
            in_specs=[vmem] * len(args),
            out_specs=[vmem] * len(out_shape) if many else vmem,
            scratch_shapes=list(scratch),
            compiler_params=PARAMS,
            cost_estimate=cost,
            name=kernel.func.__name__ if isinstance(kernel, functools.partial) else kernel.__name__,
        )(*args)

    def partial(orders, blocks, before):
        n = len(orders)
        rows = 2 * nt * ni
        kept = jax.ShapeDtypeStruct((1, 2, 2, nc, ni, width), jnp.float32)
        flops = 2 * n * rows * 2 * nb * norb * ncol * width
        out = call(
            functools.partial(part_kernel, orders),
            [kept, codes_of(4)] * n,
            [keep, *blocks, *masked],
            before,
            [pltpu.VMEM((n * rows, nb * width), jnp.bfloat16),
             pltpu.VMEM((n, 2, 2, 2, nc, ni, width), jnp.float32)],
            pl.CostEstimate(flops=flops, bytes_accessed=green_less.size * 4, transcendentals=0),
        )
        return [out[2 * at:2 * at + 2] for at in range(n)]

    def terms(n):
        return [pltpu.VMEM((n * nc, ni, width), jnp.float32)]

    def fold(state, chunk, before):
        sums, codes = state
        keep = jax.ShapeDtypeStruct((1, 2, nc, ni, width), jnp.float32)
        state = call(fold_kernel, [keep, codes_of(2)], [sums, swap(codes, chunk, 0)], before, terms(2))
        return state, state[1]

    def cross(state, chunk, before):
        sums, codes = state
        codes = call(cross_kernel, codes_of(2), [sums, swap(codes, chunk, 1)], before, terms(2))
        return codes, codes

    def final(codes, chunk, before):
        out = jax.ShapeDtypeStruct((2, nc, ni, width), jnp.bfloat16)
        out = call(final_kernel, out, [codes, swap(codes, chunk, 2)], before)
        return out, out

    def merge(mine, chunk, before):
        out = jax.ShapeDtypeStruct((2,) + mine.shape, mine.dtype)
        out = call(merge_kernel, out, [mine, swap(mine, chunk, 3)], before)
        return out, out

    def put(items, out):
        extra = [] if out is None else [out]
        n = len(items)
        return pl.pallas_call(
            functools.partial(place_kernel, [(k, ORDERS[k], last) for k, last in items]),
            out_shape=jax.ShapeDtypeStruct((nt, ncol, norb, width), jnp.bfloat16),
            in_specs=[vmem] * n + [hbm] * len(extra),
            out_specs=hbm,
            scratch_shapes=[pltpu.SemaphoreType.DMA((4 * n,))],
            input_output_aliases={n: 0} if extra else {},
            compiler_params=PARAMS,
            name="place_part",
        )(*[blocks[k][last] for k, last in items], *extra)

    state = partial(ORDERS[:2], [own_sigma, near], None)
    passed = call(copy_kernel, jax.ShapeDtypeStruct(far.shape, far.dtype), [far], state[1][1])
    state += partial(ORDERS[2:3], [far], passed)
    state += partial(ORDERS[3:], [swap_col(passed, 1)], state[2][1])
    last = state[3][1]
    todo = [[fold, cross, final, merge] for _ in range(n_col)]
    for k in STEPS:
        state[k], last = todo[k].pop(0)(state[k], k, last)
    blocks = [(state[k], swap(state[k], k, 4)) for k in range(n_col)]
    out = None
    for items in PLACES:
        out = put(items, out)
    return out


def plain(sigma_ret, sigma_less, green_less, green_adv, time_now, col_start):
    norb = green_less.shape[2]
    tb_local = green_less.shape[0]
    full_ret = lax.all_gather(sigma_ret, "col", axis=2, tiled=True)
    full_less = lax.all_gather(sigma_less, "col", axis=2, tiled=True)
    tbar = lax.axis_index("hist") * tb_local + jnp.arange(tb_local, dtype=jnp.int32)
    zero = jnp.zeros((), green_less.dtype)
    before = (tbar[None, :] <= time_now[:, None])[:, :, None, None]
    full_ret = jnp.where(before, full_ret, zero)
    full_less = jnp.where(before, full_less, zero)
    after = (tbar[:, None] >= col_start[None, :])[:, :, None, None]
    b_less = jnp.where(after, widen(green_less, norb), zero)
    b_adv = jnp.where(after, widen(green_adv, norb), zero)
    term = jnp.einsum("tbik,bckn->tcin", full_ret, b_less, preferred_element_type=jnp.float32)
    term = term + jnp.einsum("tbik,bckn->tcin", full_less, b_adv, preferred_element_type=jnp.float32)
    return lax.psum(term, "hist").astype(jnp.bfloat16)


def solution(mesh):
    n_hist, n_col = mesh.shape["hist"], mesh.shape["col"]

    def on_device(*args):
        nt, ncol = args[0].shape[0], args[2].shape[1]
        if n_hist == 8 and nt == 4 and n_col == 4 and ncol % 4 == 0 and ncol % (2 * GROUP) == 0:
            return staged(*args, n_hist, n_col)
        return plain(*args)

    return jax.shard_map(
        on_device,
        mesh=mesh,
        in_specs=(
            P(None, "hist", "col", None),
            P(None, "hist", "col", None),
            P("hist", "col", None, None),
            P("hist", "col", None, None),
            P(),
            P("col"),
        ),
        out_specs=P(None, "col", None, None),
        check_vma=False,
    )
```

```python
import functools

import jax
import jax.numpy as jnp
from jax import lax
from jax.experimental import pallas as pl
from jax.experimental.pallas import tpu as pltpu
from jax.sharding import PartitionSpec as P

BITS = {"y": 0, "z0": 1, "z1": 2}
ORDERS = ((("y", "z0", "z1", "z0", "y"), ("z0", "y", "z1", "z0", "y")), (("y", "z1", "z0", "y", "z1"), ("z1", "y", "z0", "z1", "y")), (("y", "z0", "z1", "y", "z0"), ("z0", "y", "z1", "y", "z0")), (("z1", "y", "z0", "z1", "y"), ("y", "z0", "z1", "y", "z0")))
STEPS = (0, 1, 2, 0, 3, 1, 2, 0, 3, 1, 2, 0, 3, 2, 1, 3)
PLACES = (((0, 0), (1, 0), (2, 0), (3, 0), (0, 1)), ((2, 1), (1, 1), (3, 1)))
GROUP = 3
STEPS_PER_OCTAVE = 128.0
TOP = 32512.0
LEAST = 2.0 ** -110
MIB = 2 ** 20
PARAMS = pltpu.CompilerParams(vmem_limit_bytes=40 * MIB)


def widen(green, norb):
    real_part = green[..., :norb]
    imag_part = green[..., norb:]
    lower = jnp.concatenate([-imag_part, real_part], axis=-1)
    return jnp.concatenate([green, lower], axis=-2)


def encode(read, tiles, ni, out_ref):
    rows = []
    for first in range(0, tiles, GROUP):
        values = read(first)
        most = jnp.max(jnp.max(jnp.abs(values), axis=0), axis=0, keepdims=True)
        index = jnp.ceil(jnp.log2(jnp.maximum(most, LEAST) * (1.0 / TOP)) * STEPS_PER_OCTAVE)
        codes = jnp.round(values * jnp.exp2(index * (-1.0 / STEPS_PER_OCTAVE))[None])
        out_ref[first:first + GROUP] = codes.astype(jnp.int32).astype(jnp.int16)
        rows.append(index)
    rows = rows + [jnp.zeros_like(rows[0])] * (ni - len(rows))
    out_ref[tiles] = jnp.concatenate(rows, axis=0).astype(jnp.int32).astype(jnp.int16)


def decode(in_ref, tiles):
    index = in_ref[tiles].astype(jnp.int32).astype(jnp.float32)
    scales = jnp.exp2(index * (1.0 / STEPS_PER_OCTAVE))
    return [
        in_ref[first:first + GROUP].astype(jnp.int32).astype(jnp.float32) * scales[g:g + 1][None]
        for g, first in enumerate(range(0, tiles, GROUP))
    ]


def pack_left(sigma_ref, keep_ref, left_ref, row):
    _, nt, nb, ni, width = sigma_ref.shape
    half = width // 2
    for t in range(nt):
        for b in range(nb):
            ret = sigma_ref[0, t, b] * keep_ref[t, b]
            less = sigma_ref[1, t, b] * keep_ref[t, b]
            cols = slice(b * width, (b + 1) * width)
            rows = slice(row + t * ni, row + (t + 1) * ni)
            left_ref[rows, cols] = jnp.concatenate([ret[:, :half], less[:, :half]], axis=1)
            rows = slice(row + (nt + t) * ni, row + (nt + t + 1) * ni)
            left_ref[rows, cols] = jnp.concatenate([ret[:, half:], less[:, half:]], axis=1)


def own_bits():
    hist = lax.axis_index("hist")
    bits = {d: lax.shift_right_logical(hist, at) & 1 for d, at in BITS.items()}
    return bits, lax.axis_index("col") & 1


def relative(own, core, orders, bits):
    spots = [[lax.bitwise_xor(own[d], bits[d]) for d in order] for order in orders]
    return [one if one is two else jnp.where(core == 0, one, two) for one, two in zip(*spots)]


def spots_of(orders, nt):
    own, core = own_bits()
    dims = [order[:3] for order in orders]
    return [[relative(own, core, dims, {"y": side, "z0": t % 2, "z1": t // 2}) for t in range(nt)] for side in range(2)]


def add_pair(spots, both, pair, term_ref):
    ni, width = term_ref.shape[-2:]
    half_columns = term_ref.shape[3]
    rows = both.shape[0] // 2
    lane = lax.broadcasted_iota(jnp.int32, (rows, width), 1)
    for at in range(2):
        cut = both[:, at * width:(at + 1) * width]
        turned = pltpu.roll(cut[rows:], width // 2, 1)
        value = cut[:rows] + jnp.where(lane < width // 2, -turned, turned)
        side, c = divmod(2 * pair + at, half_columns)
        for t in range(rows // ni):
            term_ref[tuple(spots[side][t]) + (c,)] = value[t * ni:(t + 1) * ni]


def part_kernel(orders, keep_ref, *refs):
    n = len(orders)
    sigma_refs, (gless_ref, gadv_ref) = refs[:n], refs[n:n + 2]
    outs, (left_ref, term_ref) = refs[-2 * n - 2:-2], refs[-2:]
    nb, ncol, norb, width = gless_ref.shape
    rows = left_ref.shape[0] // n
    for at, sigma_ref in enumerate(sigma_refs):
        pack_left(sigma_ref, keep_ref, left_ref, at * rows)
    spots = [spots_of(order, rows // (2 * term_ref.shape[-2])) for order in orders]
    for pair in range(ncol // 2):
        sides = []
        for c in (2 * pair, 2 * pair + 1):
            parts = []
            for b in range(nb):
                parts += [gless_ref[b, c], gadv_ref[b, c]]
            sides.append(jnp.concatenate(parts, axis=0))
        both = jnp.dot(left_ref[...], jnp.concatenate(sides, axis=1), preferred_element_type=jnp.float32)
        for at in range(n):
            add_pair(spots[at], both[at * rows:(at + 1) * rows], pair, term_ref.at[at])
    for at in range(n):
        kept_ref, out_ref = outs[2 * at:2 * at + 2]
        _, n1, n2, half_columns, ni, _ = term_ref.shape[1:]
        kept_ref[0] = term_ref[at, 0]

        def read(first):
            block, c = divmod(first, half_columns)
            a, b = divmod(block, n2)
            return term_ref[at, 1, a, b, c:c + GROUP]

        encode(read, n1 * n2 * half_columns, ni, out_ref)


def fold_kernel(sum_ref, in_ref, *refs):
    keep_ref, out_ref, term_ref = refs[-3:]
    _, nd, nc, ni, width = keep_ref.shape
    tiles = nd * nc
    came = decode(in_ref, 2 * tiles)
    for g, first in enumerate(range(0, tiles, GROUP)):
        d, c = divmod(first, nc)
        keep_ref[0, d, c:c + GROUP] = sum_ref[0, 0, d, c:c + GROUP] + came[g]
        term_ref[first:first + GROUP] = sum_ref[0, 1, d, c:c + GROUP] + came[g + tiles // GROUP]
    encode(lambda first: term_ref[first:first + GROUP], tiles, ni, out_ref)


def cross_kernel(sum_ref, in_ref, *refs):
    out_ref, term_ref = refs[-2:]
    _, nd, nc, ni, width = sum_ref.shape
    for g, came in enumerate(decode(in_ref, nd * nc)):
        d, c = divmod(g * GROUP, nc)
        term_ref[g * GROUP:(g + 1) * GROUP] = sum_ref[0, d, c:c + GROUP] + came
    encode(lambda first: term_ref[first:first + GROUP], nd * nc, ni, out_ref)


def final_kernel(mine_ref, other_ref, *refs):
    out_ref = refs[-1]
    nd, nc, ni, width = out_ref.shape
    mine, other = decode(mine_ref, nd * nc), decode(other_ref, nd * nc)
    half = len(mine) // 2
    for g in range(len(mine)):
        d, c = divmod(g * GROUP, nc)
        out_ref[d, c:c + GROUP] = (mine[g] + other[(g + half) % len(mine)]).astype(jnp.bfloat16)


def merge_kernel(mine_ref, other_ref, *refs):
    out_ref = refs[-1]
    out_ref[0] = mine_ref[...]
    out_ref[1] = other_ref[...]


def copy_kernel(in_ref, *refs):
    refs[-1][...] = in_ref[...]


def place_kernel(items, *refs):
    blocks, out_ref, sem = refs[:len(items)], refs[-2], refs[-1]
    own, core = own_bits()
    copies = []
    for block, (chunk, orders, last) in zip(blocks, items):
        nc, ni, _ = block.shape[-3:]
        row = pl.multiple_of(lax.bitwise_xor(lax.axis_index("col"), chunk) * ni, ni)
        for second in range(2):
            for first in range(2):
                places = []
                for order in orders:
                    bits = dict(zip(order[2:], (first, second, last)))
                    places.append([lax.bitwise_xor(own[d], bits[d]) for d in ("y", "z0", "z1")])
                y, z0, z1 = (jnp.where(core == 0, *pair) for pair in zip(*places))
                target = out_ref.at[2 * z1 + z0, pl.ds(y * nc, nc), pl.ds(row, ni)]
                copies.append(pltpu.make_async_copy(block.at[second, first], target, sem.at[len(copies)]))
    for copy in copies:
        copy.start()
    for copy in copies:
        copy.wait()


def staged(sigma_ret, sigma_less, green_less, green_adv, time_now, col_start, n_hist, n_col):
    nt, nb, ni, width = sigma_ret.shape
    _, ncol, norb, _ = green_less.shape
    nc = ncol // 2
    hist = lax.axis_index("hist")
    def swap(v, chunk, stage):
        pairs = []
        for h in range(n_hist):
            for c in range(n_col):
                partner = h ^ (1 << BITS[ORDERS[chunk][c % 2][stage]])
                pairs.append((h * n_col + c, partner * n_col + c))
        return lax.ppermute(v, ("hist", "col"), pairs)

    def swap_col(v, k):
        return lax.ppermute(v, "col", [(i, i ^ k) for i in range(n_col)])

    vmem = pl.BlockSpec(memory_space=pltpu.VMEM)
    hbm = pl.BlockSpec(memory_space=pltpu.HBM)

    def codes_of(n):
        return jax.ShapeDtypeStruct((n * nc + 1, ni, width), jnp.int16)

    own_sigma = jnp.stack([sigma_ret, sigma_less])
    tbar = hist * nb + jnp.arange(nb, dtype=jnp.int32)
    after = (tbar[:, None] >= col_start[None, :])[:, :, None, None]
    zero = jnp.zeros((), green_less.dtype)
    before = (tbar[None, :] <= time_now[:, None]).astype(sigma_ret.dtype)
    keep = jnp.broadcast_to(before[:, :, None, None], sigma_ret.shape)
    masked = [jnp.where(after, green, zero) for green in (green_less, green_adv)]
    near = swap_col(own_sigma, 1)
    far = swap_col(own_sigma, 2)

    def call(kernel, out_shape, args, before, scratch=(), cost=None):
        args = list(args) + ([] if before is None else [before])
        many = isinstance(out_shape, list)
        return pl.pallas_call(
            kernel,
            out_shape=out_shape,
            in_specs=[vmem] * len(args),
            out_specs=[vmem] * len(out_shape) if many else vmem,
            scratch_shapes=list(scratch),
            compiler_params=PARAMS,
            cost_estimate=cost,
            name=kernel.func.__name__ if isinstance(kernel, functools.partial) else kernel.__name__,
        )(*args)

    def partial(orders, blocks, before):
        n = len(orders)
        rows = 2 * nt * ni
        kept = jax.ShapeDtypeStruct((1, 2, 2, nc, ni, width), jnp.float32)
        flops = 2 * n * rows * 2 * nb * norb * ncol * width
        out = call(
            functools.partial(part_kernel, orders),
            [kept, codes_of(4)] * n,
            [keep, *blocks, *masked],
            before,
            [pltpu.VMEM((n * rows, nb * width), jnp.bfloat16),
             pltpu.VMEM((n, 2, 2, 2, nc, ni, width), jnp.float32)],
            pl.CostEstimate(flops=flops, bytes_accessed=green_less.size * 4, transcendentals=0),
        )
        return [out[2 * at:2 * at + 2] for at in range(n)]

    def terms(n):
        return [pltpu.VMEM((n * nc, ni, width), jnp.float32)]

    def fold(state, chunk, before):
        sums, codes = state
        keep = jax.ShapeDtypeStruct((1, 2, nc, ni, width), jnp.float32)
        state = call(fold_kernel, [keep, codes_of(2)], [sums, swap(codes, chunk, 0)], before, terms(2))
        return state, state[1]

    def cross(state, chunk, before):
        sums, codes = state
        codes = call(cross_kernel, codes_of(2), [sums, swap(codes, chunk, 1)], before, terms(2))
        return codes, codes

    def final(codes, chunk, before):
        out = jax.ShapeDtypeStruct((2, nc, ni, width), jnp.bfloat16)
        out = call(final_kernel, out, [codes, swap(codes, chunk, 2)], before)
        return out, out

    def merge(mine, chunk, before):
        out = jax.ShapeDtypeStruct((2,) + mine.shape, mine.dtype)
        out = call(merge_kernel, out, [mine, swap(mine, chunk, 3)], before)
        return out, out

    def put(items, out):
        extra = [] if out is None else [out]
        n = len(items)
        return pl.pallas_call(
            functools.partial(place_kernel, [(k, ORDERS[k], last) for k, last in items]),
            out_shape=jax.ShapeDtypeStruct((nt, ncol, norb, width), jnp.bfloat16),
            in_specs=[vmem] * n + [hbm] * len(extra),
            out_specs=hbm,
            scratch_shapes=[pltpu.SemaphoreType.DMA((4 * n,))],
            input_output_aliases={n: 0} if extra else {},
            compiler_params=PARAMS,
            name="place_part",
        )(*[blocks[k][last] for k, last in items], *extra)

    state = partial(ORDERS[:2], [own_sigma, near], None)
    passed = call(copy_kernel, jax.ShapeDtypeStruct(far.shape, far.dtype), [far], state[1][1])
    state += partial(ORDERS[2:3], [far], passed)
    state += partial(ORDERS[3:], [swap_col(passed, 1)], state[2][1])
    last = state[3][1]
    todo = [[fold, cross, final, merge] for _ in range(n_col)]
    for k in STEPS:
        state[k], last = todo[k].pop(0)(state[k], k, last)
    blocks = [(state[k], swap(state[k], k, 4)) for k in range(n_col)]
    out = None
    for items in PLACES:
        out = put(items, out)
    return out


def plain(sigma_ret, sigma_less, green_less, green_adv, time_now, col_start):
    norb = green_less.shape[2]
    tb_local = green_less.shape[0]
    full_ret = lax.all_gather(sigma_ret, "col", axis=2, tiled=True)
    full_less = lax.all_gather(sigma_less, "col", axis=2, tiled=True)
    tbar = lax.axis_index("hist") * tb_local + jnp.arange(tb_local, dtype=jnp.int32)
    zero = jnp.zeros((), green_less.dtype)
    before = (tbar[None, :] <= time_now[:, None])[:, :, None, None]
    full_ret = jnp.where(before, full_ret, zero)
    full_less = jnp.where(before, full_less, zero)
    after = (tbar[:, None] >= col_start[None, :])[:, :, None, None]
    b_less = jnp.where(after, widen(green_less, norb), zero)
    b_adv = jnp.where(after, widen(green_adv, norb), zero)
    term = jnp.einsum("tbik,bckn->tcin", full_ret, b_less, preferred_element_type=jnp.float32)
    term = term + jnp.einsum("tbik,bckn->tcin", full_less, b_adv, preferred_element_type=jnp.float32)
    return lax.psum(term, "hist").astype(jnp.bfloat16)


def solution(mesh):
    n_hist, n_col = mesh.shape["hist"], mesh.shape["col"]

    def on_device(*args):
        nt, ncol = args[0].shape[0], args[2].shape[1]
        if n_hist == 8 and nt == 4 and n_col == 4 and ncol % 4 == 0 and ncol % (2 * GROUP) == 0:
            return staged(*args, n_hist, n_col)
        return plain(*args)

    return jax.shard_map(
        on_device,
        mesh=mesh,
        in_specs=(
            P(None, "hist", "col", None),
            P(None, "hist", "col", None),
            P("hist", "col", None, None),
            P("hist", "col", None, None),
            P(),
            P("col"),
        ),
        out_specs=P(None, "col", None, None),
        check_vma=False,
    )
```

```python
import functools

import jax
import jax.numpy as jnp
from jax import lax
from jax.experimental import pallas as pl
from jax.experimental.pallas import tpu as pltpu
from jax.sharding import PartitionSpec as P

BITS = {"y": 0, "z0": 1, "z1": 2}
ORDERS = ((("y", "z0", "z1", "z0", "y"), ("z0", "y", "z1", "z0", "y")), (("y", "z1", "z0", "z1", "y"), ("z1", "y", "z0", "y", "z1")), (("y", "z0", "z1", "y", "z0"), ("z0", "y", "z1", "y", "z0")), (("z1", "y", "z0", "z1", "y"), ("y", "z0", "z1", "y", "z0")))
STEPS = (0, 1, 2, 0, 3, 1, 2, 0, 3, 1, 2, 0, 3, 2, 1, 3)
PLACES = (((0, 0), (1, 0), (2, 0), (3, 0), (0, 1)), ((2, 1), (1, 1), (3, 1)))
GROUP = 3
STEPS_PER_OCTAVE = 128.0
TOP = 32512.0
LEAST = 2.0 ** -110
MIB = 2 ** 20
PARAMS = pltpu.CompilerParams(vmem_limit_bytes=40 * MIB)


def widen(green, norb):
    real_part = green[..., :norb]
    imag_part = green[..., norb:]
    lower = jnp.concatenate([-imag_part, real_part], axis=-1)
    return jnp.concatenate([green, lower], axis=-2)


def encode(read, tiles, ni, out_ref):
    rows = []
    for first in range(0, tiles, GROUP):
        values = read(first)
        most = jnp.max(jnp.max(jnp.abs(values), axis=0), axis=0, keepdims=True)
        index = jnp.ceil(jnp.log2(jnp.maximum(most, LEAST) * (1.0 / TOP)) * STEPS_PER_OCTAVE)
        codes = jnp.round(values * jnp.exp2(index * (-1.0 / STEPS_PER_OCTAVE))[None])
        out_ref[first:first + GROUP] = codes.astype(jnp.int32).astype(jnp.int16)
        rows.append(index)
    rows = rows + [jnp.zeros_like(rows[0])] * (ni - len(rows))
    out_ref[tiles] = jnp.concatenate(rows, axis=0).astype(jnp.int32).astype(jnp.int16)


def decode(in_ref, tiles):
    index = in_ref[tiles].astype(jnp.int32).astype(jnp.float32)
    scales = jnp.exp2(index * (1.0 / STEPS_PER_OCTAVE))
    return [
        in_ref[first:first + GROUP].astype(jnp.int32).astype(jnp.float32) * scales[g:g + 1][None]
        for g, first in enumerate(range(0, tiles, GROUP))
    ]


def pack_left(sigma_ref, keep_ref, left_ref, row):
    _, nt, nb, ni, width = sigma_ref.shape
    half = width // 2
    for t in range(nt):
        for b in range(nb):
            ret = sigma_ref[0, t, b] * keep_ref[t, b]
            less = sigma_ref[1, t, b] * keep_ref[t, b]
            cols = slice(b * width, (b + 1) * width)
            rows = slice(row + t * ni, row + (t + 1) * ni)
            left_ref[rows, cols] = jnp.concatenate([ret[:, :half], less[:, :half]], axis=1)
            rows = slice(row + (nt + t) * ni, row + (nt + t + 1) * ni)
            left_ref[rows, cols] = jnp.concatenate([ret[:, half:], less[:, half:]], axis=1)


def own_bits():
    hist = lax.axis_index("hist")
    bits = {d: lax.shift_right_logical(hist, at) & 1 for d, at in BITS.items()}
    return bits, lax.axis_index("col") & 1


def relative(own, core, orders, bits):
    spots = [[lax.bitwise_xor(own[d], bits[d]) for d in order] for order in orders]
    return [one if one is two else jnp.where(core == 0, one, two) for one, two in zip(*spots)]


def spots_of(orders, nt):
    own, core = own_bits()
    dims = [order[:3] for order in orders]
    return [[relative(own, core, dims, {"y": side, "z0": t % 2, "z1": t // 2}) for t in range(nt)] for side in range(2)]


def add_pair(spots, both, pair, term_ref):
    ni, width = term_ref.shape[-2:]
    half_columns = term_ref.shape[3]
    rows = both.shape[0] // 2
    lane = lax.broadcasted_iota(jnp.int32, (rows, width), 1)
    for at in range(2):
        cut = both[:, at * width:(at + 1) * width]
        turned = pltpu.roll(cut[rows:], width // 2, 1)
        value = cut[:rows] + jnp.where(lane < width // 2, -turned, turned)
        side, c = divmod(2 * pair + at, half_columns)
        for t in range(rows // ni):
            term_ref[tuple(spots[side][t]) + (c,)] = value[t * ni:(t + 1) * ni]


def part_kernel(orders, keep_ref, *refs):
    n = len(orders)
    sigma_refs, (gless_ref, gadv_ref) = refs[:n], refs[n:n + 2]
    outs, (left_ref, term_ref) = refs[-2 * n - 2:-2], refs[-2:]
    nb, ncol, norb, width = gless_ref.shape
    rows = left_ref.shape[0] // n
    for at, sigma_ref in enumerate(sigma_refs):
        pack_left(sigma_ref, keep_ref, left_ref, at * rows)
    spots = [spots_of(order, rows // (2 * term_ref.shape[-2])) for order in orders]
    for pair in range(ncol // 2):
        sides = []
        for c in (2 * pair, 2 * pair + 1):
            parts = []
            for b in range(nb):
                parts += [gless_ref[b, c], gadv_ref[b, c]]
            sides.append(jnp.concatenate(parts, axis=0))
        both = jnp.dot(left_ref[...], jnp.concatenate(sides, axis=1), preferred_element_type=jnp.float32)
        for at in range(n):
            add_pair(spots[at], both[at * rows:(at + 1) * rows], pair, term_ref.at[at])
    for at in range(n):
        kept_ref, out_ref = outs[2 * at:2 * at + 2]
        _, n1, n2, half_columns, ni, _ = term_ref.shape[1:]
        kept_ref[0] = term_ref[at, 0]

        def read(first):
            block, c = divmod(first, half_columns)
            a, b = divmod(block, n2)
            return term_ref[at, 1, a, b, c:c + GROUP]

        encode(read, n1 * n2 * half_columns, ni, out_ref)


def fold_kernel(sum_ref, in_ref, *refs):
    keep_ref, out_ref, term_ref = refs[-3:]
    _, nd, nc, ni, width = keep_ref.shape
    tiles = nd * nc
    came = decode(in_ref, 2 * tiles)
    for g, first in enumerate(range(0, tiles, GROUP)):
        d, c = divmod(first, nc)
        keep_ref[0, d, c:c + GROUP] = sum_ref[0, 0, d, c:c + GROUP] + came[g]
        term_ref[first:first + GROUP] = sum_ref[0, 1, d, c:c + GROUP] + came[g + tiles // GROUP]
    encode(lambda first: term_ref[first:first + GROUP], tiles, ni, out_ref)


def cross_kernel(sum_ref, in_ref, *refs):
    out_ref, term_ref = refs[-2:]
    _, nd, nc, ni, width = sum_ref.shape
    for g, came in enumerate(decode(in_ref, nd * nc)):
        d, c = divmod(g * GROUP, nc)
        term_ref[g * GROUP:(g + 1) * GROUP] = sum_ref[0, d, c:c + GROUP] + came
    encode(lambda first: term_ref[first:first + GROUP], nd * nc, ni, out_ref)


def final_kernel(mine_ref, other_ref, *refs):
    out_ref = refs[-1]
    nd, nc, ni, width = out_ref.shape
    mine, other = decode(mine_ref, nd * nc), decode(other_ref, nd * nc)
    half = len(mine) // 2
    for g in range(len(mine)):
        d, c = divmod(g * GROUP, nc)
        out_ref[d, c:c + GROUP] = (mine[g] + other[(g + half) % len(mine)]).astype(jnp.bfloat16)


def merge_kernel(mine_ref, other_ref, *refs):
    out_ref = refs[-1]
    out_ref[0] = mine_ref[...]
    out_ref[1] = other_ref[...]


def copy_kernel(in_ref, *refs):
    refs[-1][...] = in_ref[...]


def place_kernel(items, *refs):
    blocks, out_ref, sem = refs[:len(items)], refs[-2], refs[-1]
    own, core = own_bits()
    copies = []
    for block, (chunk, orders, last) in zip(blocks, items):
        nc, ni, _ = block.shape[-3:]
        row = pl.multiple_of(lax.bitwise_xor(lax.axis_index("col"), chunk) * ni, ni)
        for second in range(2):
            for first in range(2):
                places = []
                for order in orders:
                    bits = dict(zip(order[2:], (first, second, last)))
                    places.append([lax.bitwise_xor(own[d], bits[d]) for d in ("y", "z0", "z1")])
                y, z0, z1 = (jnp.where(core == 0, *pair) for pair in zip(*places))
                target = out_ref.at[2 * z1 + z0, pl.ds(y * nc, nc), pl.ds(row, ni)]
                copies.append(pltpu.make_async_copy(block.at[second, first], target, sem.at[len(copies)]))
    for copy in copies:
        copy.start()
    for copy in copies:
        copy.wait()


def staged(sigma_ret, sigma_less, green_less, green_adv, time_now, col_start, n_hist, n_col):
    nt, nb, ni, width = sigma_ret.shape
    _, ncol, norb, _ = green_less.shape
    nc = ncol // 2
    hist = lax.axis_index("hist")
    def swap(v, chunk, stage):
        pairs = []
        for h in range(n_hist):
            for c in range(n_col):
                partner = h ^ (1 << BITS[ORDERS[chunk][c % 2][stage]])
                pairs.append((h * n_col + c, partner * n_col + c))
        return lax.ppermute(v, ("hist", "col"), pairs)

    def swap_col(v, k):
        return lax.ppermute(v, "col", [(i, i ^ k) for i in range(n_col)])

    vmem = pl.BlockSpec(memory_space=pltpu.VMEM)
    hbm = pl.BlockSpec(memory_space=pltpu.HBM)

    def codes_of(n):
        return jax.ShapeDtypeStruct((n * nc + 1, ni, width), jnp.int16)

    own_sigma = jnp.stack([sigma_ret, sigma_less])
    tbar = hist * nb + jnp.arange(nb, dtype=jnp.int32)
    after = (tbar[:, None] >= col_start[None, :])[:, :, None, None]
    zero = jnp.zeros((), green_less.dtype)
    before = (tbar[None, :] <= time_now[:, None]).astype(sigma_ret.dtype)
    keep = jnp.broadcast_to(before[:, :, None, None], sigma_ret.shape)
    masked = [jnp.where(after, green, zero) for green in (green_less, green_adv)]
    near = swap_col(own_sigma, 1)
    far = swap_col(own_sigma, 2)

    def call(kernel, out_shape, args, before, scratch=(), cost=None):
        args = list(args) + ([] if before is None else [before])
        many = isinstance(out_shape, list)
        return pl.pallas_call(
            kernel,
            out_shape=out_shape,
            in_specs=[vmem] * len(args),
            out_specs=[vmem] * len(out_shape) if many else vmem,
            scratch_shapes=list(scratch),
            compiler_params=PARAMS,
            cost_estimate=cost,
            name=kernel.func.__name__ if isinstance(kernel, functools.partial) else kernel.__name__,
        )(*args)

    def partial(orders, blocks, before):
        n = len(orders)
        rows = 2 * nt * ni
        kept = jax.ShapeDtypeStruct((1, 2, 2, nc, ni, width), jnp.float32)
        flops = 2 * n * rows * 2 * nb * norb * ncol * width
        out = call(
            functools.partial(part_kernel, orders),
            [kept, codes_of(4)] * n,
            [keep, *blocks, *masked],
            before,
            [pltpu.VMEM((n * rows, nb * width), jnp.bfloat16),
             pltpu.VMEM((n, 2, 2, 2, nc, ni, width), jnp.float32)],
            pl.CostEstimate(flops=flops, bytes_accessed=green_less.size * 4, transcendentals=0),
        )
        return [out[2 * at:2 * at + 2] for at in range(n)]

    def terms(n):
        return [pltpu.VMEM((n * nc, ni, width), jnp.float32)]

    def fold(state, chunk, before):
        sums, codes = state
        keep = jax.ShapeDtypeStruct((1, 2, nc, ni, width), jnp.float32)
        state = call(fold_kernel, [keep, codes_of(2)], [sums, swap(codes, chunk, 0)], before, terms(2))
        return state, state[1]

    def cross(state, chunk, before):
        sums, codes = state
        codes = call(cross_kernel, codes_of(2), [sums, swap(codes, chunk, 1)], before, terms(2))
        return codes, codes

    def final(codes, chunk, before):
        out = jax.ShapeDtypeStruct((2, nc, ni, width), jnp.bfloat16)
        out = call(final_kernel, out, [codes, swap(codes, chunk, 2)], before)
        return out, out

    def merge(mine, chunk, before):
        out = jax.ShapeDtypeStruct((2,) + mine.shape, mine.dtype)
        out = call(merge_kernel, out, [mine, swap(mine, chunk, 3)], before)
        return out, out

    def put(items, out):
        extra = [] if out is None else [out]
        n = len(items)
        return pl.pallas_call(
            functools.partial(place_kernel, [(k, ORDERS[k], last) for k, last in items]),
            out_shape=jax.ShapeDtypeStruct((nt, ncol, norb, width), jnp.bfloat16),
            in_specs=[vmem] * n + [hbm] * len(extra),
            out_specs=hbm,
            scratch_shapes=[pltpu.SemaphoreType.DMA((4 * n,))],
            input_output_aliases={n: 0} if extra else {},
            compiler_params=PARAMS,
            name="place_part",
        )(*[blocks[k][last] for k, last in items], *extra)

    state = partial(ORDERS[:2], [own_sigma, near], None)
    passed = call(copy_kernel, jax.ShapeDtypeStruct(far.shape, far.dtype), [far], state[1][1])
    state += partial(ORDERS[2:3], [far], passed)
    state += partial(ORDERS[3:], [swap_col(passed, 1)], state[2][1])
    last = state[3][1]
    todo = [[fold, cross, final, merge] for _ in range(n_col)]
    for k in STEPS:
        state[k], last = todo[k].pop(0)(state[k], k, last)
    blocks = [(state[k], swap(state[k], k, 4)) for k in range(n_col)]
    out = None
    for items in PLACES:
        out = put(items, out)
    return out


def plain(sigma_ret, sigma_less, green_less, green_adv, time_now, col_start):
    norb = green_less.shape[2]
    tb_local = green_less.shape[0]
    full_ret = lax.all_gather(sigma_ret, "col", axis=2, tiled=True)
    full_less = lax.all_gather(sigma_less, "col", axis=2, tiled=True)
    tbar = lax.axis_index("hist") * tb_local + jnp.arange(tb_local, dtype=jnp.int32)
    zero = jnp.zeros((), green_less.dtype)
    before = (tbar[None, :] <= time_now[:, None])[:, :, None, None]
    full_ret = jnp.where(before, full_ret, zero)
    full_less = jnp.where(before, full_less, zero)
    after = (tbar[:, None] >= col_start[None, :])[:, :, None, None]
    b_less = jnp.where(after, widen(green_less, norb), zero)
    b_adv = jnp.where(after, widen(green_adv, norb), zero)
    term = jnp.einsum("tbik,bckn->tcin", full_ret, b_less, preferred_element_type=jnp.float32)
    term = term + jnp.einsum("tbik,bckn->tcin", full_less, b_adv, preferred_element_type=jnp.float32)
    return lax.psum(term, "hist").astype(jnp.bfloat16)


def solution(mesh):
    n_hist, n_col = mesh.shape["hist"], mesh.shape["col"]

    def on_device(*args):
        nt, ncol = args[0].shape[0], args[2].shape[1]
        if n_hist == 8 and nt == 4 and n_col == 4 and ncol % 4 == 0 and ncol % (2 * GROUP) == 0:
            return staged(*args, n_hist, n_col)
        return plain(*args)

    return jax.shard_map(
        on_device,
        mesh=mesh,
        in_specs=(
            P(None, "hist", "col", None),
            P(None, "hist", "col", None),
            P("hist", "col", None, None),
            P("hist", "col", None, None),
            P(),
            P("col"),
        ),
        out_specs=P(None, "col", None, None),
        check_vma=False,
    )
```

```python
import functools

import jax
import jax.numpy as jnp
from jax import lax
from jax.experimental import pallas as pl
from jax.experimental.pallas import tpu as pltpu
from jax.sharding import PartitionSpec as P

BITS = {"y": 0, "z0": 1, "z1": 2}
ORDERS = ((("y", "z0", "z1", "z0", "y"), ("z0", "y", "z1", "z0", "y")), (("y", "z1", "z0", "y", "z1"), ("z1", "y", "z0", "z1", "y")), (("y", "z0", "z1", "y", "z0"), ("z0", "y", "z1", "z0", "y")), (("z1", "y", "z0", "z1", "y"), ("y", "z0", "z1", "y", "z0")))
STEPS = (0, 1, 2, 0, 3, 1, 2, 0, 3, 1, 2, 0, 3, 1, 2, 3)
PLACES = (((0, 0), (1, 0), (2, 0), (3, 0), (0, 1)), ((1, 1), (2, 1), (3, 1)))
GROUP = 3
STEPS_PER_OCTAVE = 128.0
TOP = 32512.0
LEAST = 2.0 ** -110
MIB = 2 ** 20
PARAMS = pltpu.CompilerParams(vmem_limit_bytes=40 * MIB)


def widen(green, norb):
    real_part = green[..., :norb]
    imag_part = green[..., norb:]
    lower = jnp.concatenate([-imag_part, real_part], axis=-1)
    return jnp.concatenate([green, lower], axis=-2)


def encode(read, tiles, ni, out_ref):
    rows = []
    for first in range(0, tiles, GROUP):
        values = read(first)
        most = jnp.max(jnp.max(jnp.abs(values), axis=0), axis=0, keepdims=True)
        index = jnp.ceil(jnp.log2(jnp.maximum(most, LEAST) * (1.0 / TOP)) * STEPS_PER_OCTAVE)
        codes = jnp.round(values * jnp.exp2(index * (-1.0 / STEPS_PER_OCTAVE))[None])
        out_ref[first:first + GROUP] = codes.astype(jnp.int32).astype(jnp.int16)
        rows.append(index)
    rows = rows + [jnp.zeros_like(rows[0])] * (ni - len(rows))
    out_ref[tiles] = jnp.concatenate(rows, axis=0).astype(jnp.int32).astype(jnp.int16)


def decode(in_ref, tiles):
    index = in_ref[tiles].astype(jnp.int32).astype(jnp.float32)
    scales = jnp.exp2(index * (1.0 / STEPS_PER_OCTAVE))
    return [
        in_ref[first:first + GROUP].astype(jnp.int32).astype(jnp.float32) * scales[g:g + 1][None]
        for g, first in enumerate(range(0, tiles, GROUP))
    ]


def pack_left(sigma_ref, keep_ref, left_ref, row):
    _, nt, nb, ni, width = sigma_ref.shape
    half = width // 2
    for t in range(nt):
        for b in range(nb):
            ret = sigma_ref[0, t, b] * keep_ref[t, b]
            less = sigma_ref[1, t, b] * keep_ref[t, b]
            cols = slice(b * width, (b + 1) * width)
            rows = slice(row + t * ni, row + (t + 1) * ni)
            left_ref[rows, cols] = jnp.concatenate([ret[:, :half], less[:, :half]], axis=1)
            rows = slice(row + (nt + t) * ni, row + (nt + t + 1) * ni)
            left_ref[rows, cols] = jnp.concatenate([ret[:, half:], less[:, half:]], axis=1)


def own_bits():
    hist = lax.axis_index("hist")
    bits = {d: lax.shift_right_logical(hist, at) & 1 for d, at in BITS.items()}
    return bits, lax.axis_index("col") & 1


def relative(own, core, orders, bits):
    spots = [[lax.bitwise_xor(own[d], bits[d]) for d in order] for order in orders]
    return [one if one is two else jnp.where(core == 0, one, two) for one, two in zip(*spots)]


def spots_of(orders, nt):
    own, core = own_bits()
    dims = [order[:3] for order in orders]
    return [[relative(own, core, dims, {"y": side, "z0": t % 2, "z1": t // 2}) for t in range(nt)] for side in range(2)]


def add_pair(spots, both, pair, term_ref):
    ni, width = term_ref.shape[-2:]
    half_columns = term_ref.shape[3]
    rows = both.shape[0] // 2
    lane = lax.broadcasted_iota(jnp.int32, (rows, width), 1)
    for at in range(2):
        cut = both[:, at * width:(at + 1) * width]
        turned = pltpu.roll(cut[rows:], width // 2, 1)
        value = cut[:rows] + jnp.where(lane < width // 2, -turned, turned)
        side, c = divmod(2 * pair + at, half_columns)
        for t in range(rows // ni):
            term_ref[tuple(spots[side][t]) + (c,)] = value[t * ni:(t + 1) * ni]


def part_kernel(orders, keep_ref, *refs):
    n = len(orders)
    sigma_refs, (gless_ref, gadv_ref) = refs[:n], refs[n:n + 2]
    outs, (left_ref, term_ref) = refs[-2 * n - 2:-2], refs[-2:]
    nb, ncol, norb, width = gless_ref.shape
    rows = left_ref.shape[0] // n
    for at, sigma_ref in enumerate(sigma_refs):
        pack_left(sigma_ref, keep_ref, left_ref, at * rows)
    spots = [spots_of(order, rows // (2 * term_ref.shape[-2])) for order in orders]
    for pair in range(ncol // 2):
        sides = []
        for c in (2 * pair, 2 * pair + 1):
            parts = []
            for b in range(nb):
                parts += [gless_ref[b, c], gadv_ref[b, c]]
            sides.append(jnp.concatenate(parts, axis=0))
        both = jnp.dot(left_ref[...], jnp.concatenate(sides, axis=1), preferred_element_type=jnp.float32)
        for at in range(n):
            add_pair(spots[at], both[at * rows:(at + 1) * rows], pair, term_ref.at[at])
    for at in range(n):
        kept_ref, out_ref = outs[2 * at:2 * at + 2]
        _, n1, n2, half_columns, ni, _ = term_ref.shape[1:]
        kept_ref[0] = term_ref[at, 0]

        def read(first):
            block, c = divmod(first, half_columns)
            a, b = divmod(block, n2)
            return term_ref[at, 1, a, b, c:c + GROUP]

        encode(read, n1 * n2 * half_columns, ni, out_ref)


def fold_kernel(sum_ref, in_ref, *refs):
    keep_ref, out_ref, term_ref = refs[-3:]
    _, nd, nc, ni, width = keep_ref.shape
    tiles = nd * nc
    came = decode(in_ref, 2 * tiles)
    for g, first in enumerate(range(0, tiles, GROUP)):
        d, c = divmod(first, nc)
        keep_ref[0, d, c:c + GROUP] = sum_ref[0, 0, d, c:c + GROUP] + came[g]
        term_ref[first:first + GROUP] = sum_ref[0, 1, d, c:c + GROUP] + came[g + tiles // GROUP]
    encode(lambda first: term_ref[first:first + GROUP], tiles, ni, out_ref)


def cross_kernel(sum_ref, in_ref, *refs):
    out_ref, term_ref = refs[-2:]
    _, nd, nc, ni, width = sum_ref.shape
    for g, came in enumerate(decode(in_ref, nd * nc)):
        d, c = divmod(g * GROUP, nc)
        term_ref[g * GROUP:(g + 1) * GROUP] = sum_ref[0, d, c:c + GROUP] + came
    encode(lambda first: term_ref[first:first + GROUP], nd * nc, ni, out_ref)


def final_kernel(mine_ref, other_ref, *refs):
    out_ref = refs[-1]
    nd, nc, ni, width = out_ref.shape
    mine, other = decode(mine_ref, nd * nc), decode(other_ref, nd * nc)
    half = len(mine) // 2
    for g in range(len(mine)):
        d, c = divmod(g * GROUP, nc)
        out_ref[d, c:c + GROUP] = (mine[g] + other[(g + half) % len(mine)]).astype(jnp.bfloat16)


def merge_kernel(mine_ref, other_ref, *refs):
    out_ref = refs[-1]
    out_ref[0] = mine_ref[...]
    out_ref[1] = other_ref[...]


def copy_kernel(in_ref, *refs):
    refs[-1][...] = in_ref[...]


def place_kernel(items, *refs):
    blocks, out_ref, sem = refs[:len(items)], refs[-2], refs[-1]
    own, core = own_bits()
    copies = []
    for block, (chunk, orders, last) in zip(blocks, items):
        nc, ni, _ = block.shape[-3:]
        row = pl.multiple_of(lax.bitwise_xor(lax.axis_index("col"), chunk) * ni, ni)
        for second in range(2):
            for first in range(2):
                places = []
                for order in orders:
                    bits = dict(zip(order[2:], (first, second, last)))
                    places.append([lax.bitwise_xor(own[d], bits[d]) for d in ("y", "z0", "z1")])
                y, z0, z1 = (jnp.where(core == 0, *pair) for pair in zip(*places))
                target = out_ref.at[2 * z1 + z0, pl.ds(y * nc, nc), pl.ds(row, ni)]
                copies.append(pltpu.make_async_copy(block.at[second, first], target, sem.at[len(copies)]))
    for copy in copies:
        copy.start()
    for copy in copies:
        copy.wait()


def staged(sigma_ret, sigma_less, green_less, green_adv, time_now, col_start, n_hist, n_col):
    nt, nb, ni, width = sigma_ret.shape
    _, ncol, norb, _ = green_less.shape
    nc = ncol // 2
    hist = lax.axis_index("hist")
    def swap(v, chunk, stage):
        pairs = []
        for h in range(n_hist):
            for c in range(n_col):
                partner = h ^ (1 << BITS[ORDERS[chunk][c % 2][stage]])
                pairs.append((h * n_col + c, partner * n_col + c))
        return lax.ppermute(v, ("hist", "col"), pairs)

    def swap_col(v, k):
        return lax.ppermute(v, "col", [(i, i ^ k) for i in range(n_col)])

    vmem = pl.BlockSpec(memory_space=pltpu.VMEM)
    hbm = pl.BlockSpec(memory_space=pltpu.HBM)

    def codes_of(n):
        return jax.ShapeDtypeStruct((n * nc + 1, ni, width), jnp.int16)

    own_sigma = jnp.stack([sigma_ret, sigma_less])
    tbar = hist * nb + jnp.arange(nb, dtype=jnp.int32)
    after = (tbar[:, None] >= col_start[None, :])[:, :, None, None]
    zero = jnp.zeros((), green_less.dtype)
    before = (tbar[None, :] <= time_now[:, None]).astype(sigma_ret.dtype)
    keep = jnp.broadcast_to(before[:, :, None, None], sigma_ret.shape)
    masked = [jnp.where(after, green, zero) for green in (green_less, green_adv)]
    near = swap_col(own_sigma, 1)
    far = swap_col(own_sigma, 2)

    def call(kernel, out_shape, args, before, scratch=(), cost=None):
        args = list(args) + ([] if before is None else [before])
        many = isinstance(out_shape, list)
        return pl.pallas_call(
            kernel,
            out_shape=out_shape,
            in_specs=[vmem] * len(args),
            out_specs=[vmem] * len(out_shape) if many else vmem,
            scratch_shapes=list(scratch),
            compiler_params=PARAMS,
            cost_estimate=cost,
            name=kernel.func.__name__ if isinstance(kernel, functools.partial) else kernel.__name__,
        )(*args)

    def partial(orders, blocks, before):
        n = len(orders)
        rows = 2 * nt * ni
        kept = jax.ShapeDtypeStruct((1, 2, 2, nc, ni, width), jnp.float32)
        flops = 2 * n * rows * 2 * nb * norb * ncol * width
        out = call(
            functools.partial(part_kernel, orders),
            [kept, codes_of(4)] * n,
            [keep, *blocks, *masked],
            before,
            [pltpu.VMEM((n * rows, nb * width), jnp.bfloat16),
             pltpu.VMEM((n, 2, 2, 2, nc, ni, width), jnp.float32)],
            pl.CostEstimate(flops=flops, bytes_accessed=green_less.size * 4, transcendentals=0),
        )
        return [out[2 * at:2 * at + 2] for at in range(n)]

    def terms(n):
        return [pltpu.VMEM((n * nc, ni, width), jnp.float32)]

    def fold(state, chunk, before):
        sums, codes = state
        keep = jax.ShapeDtypeStruct((1, 2, nc, ni, width), jnp.float32)
        state = call(fold_kernel, [keep, codes_of(2)], [sums, swap(codes, chunk, 0)], before, terms(2))
        return state, state[1]

    def cross(state, chunk, before):
        sums, codes = state
        codes = call(cross_kernel, codes_of(2), [sums, swap(codes, chunk, 1)], before, terms(2))
        return codes, codes

    def final(codes, chunk, before):
        out = jax.ShapeDtypeStruct((2, nc, ni, width), jnp.bfloat16)
        out = call(final_kernel, out, [codes, swap(codes, chunk, 2)], before)
        return out, out

    def merge(mine, chunk, before):
        out = jax.ShapeDtypeStruct((2,) + mine.shape, mine.dtype)
        out = call(merge_kernel, out, [mine, swap(mine, chunk, 3)], before)
        return out, out

    def put(items, out):
        extra = [] if out is None else [out]
        n = len(items)
        return pl.pallas_call(
            functools.partial(place_kernel, [(k, ORDERS[k], last) for k, last in items]),
            out_shape=jax.ShapeDtypeStruct((nt, ncol, norb, width), jnp.bfloat16),
            in_specs=[vmem] * n + [hbm] * len(extra),
            out_specs=hbm,
            scratch_shapes=[pltpu.SemaphoreType.DMA((4 * n,))],
            input_output_aliases={n: 0} if extra else {},
            compiler_params=PARAMS,
            name="place_part",
        )(*[blocks[k][last] for k, last in items], *extra)

    state = partial(ORDERS[:2], [own_sigma, near], None)
    passed = call(copy_kernel, jax.ShapeDtypeStruct(far.shape, far.dtype), [far], state[1][1])
    state += partial(ORDERS[2:3], [far], passed)
    state += partial(ORDERS[3:], [swap_col(passed, 1)], state[2][1])
    last = state[3][1]
    todo = [[fold, cross, final, merge] for _ in range(n_col)]
    for k in STEPS:
        state[k], last = todo[k].pop(0)(state[k], k, last)
    blocks = [(state[k], swap(state[k], k, 4)) for k in range(n_col)]
    out = None
    for items in PLACES:
        out = put(items, out)
    return out


def plain(sigma_ret, sigma_less, green_less, green_adv, time_now, col_start):
    norb = green_less.shape[2]
    tb_local = green_less.shape[0]
    full_ret = lax.all_gather(sigma_ret, "col", axis=2, tiled=True)
    full_less = lax.all_gather(sigma_less, "col", axis=2, tiled=True)
    tbar = lax.axis_index("hist") * tb_local + jnp.arange(tb_local, dtype=jnp.int32)
    zero = jnp.zeros((), green_less.dtype)
    before = (tbar[None, :] <= time_now[:, None])[:, :, None, None]
    full_ret = jnp.where(before, full_ret, zero)
    full_less = jnp.where(before, full_less, zero)
    after = (tbar[:, None] >= col_start[None, :])[:, :, None, None]
    b_less = jnp.where(after, widen(green_less, norb), zero)
    b_adv = jnp.where(after, widen(green_adv, norb), zero)
    term = jnp.einsum("tbik,bckn->tcin", full_ret, b_less, preferred_element_type=jnp.float32)
    term = term + jnp.einsum("tbik,bckn->tcin", full_less, b_adv, preferred_element_type=jnp.float32)
    return lax.psum(term, "hist").astype(jnp.bfloat16)


def solution(mesh):
    n_hist, n_col = mesh.shape["hist"], mesh.shape["col"]

    def on_device(*args):
        nt, ncol = args[0].shape[0], args[2].shape[1]
        if n_hist == 8 and nt == 4 and n_col == 4 and ncol % 4 == 0 and ncol % (2 * GROUP) == 0:
            return staged(*args, n_hist, n_col)
        return plain(*args)

    return jax.shard_map(
        on_device,
        mesh=mesh,
        in_specs=(
            P(None, "hist", "col", None),
            P(None, "hist", "col", None),
            P("hist", "col", None, None),
            P("hist", "col", None, None),
            P(),
            P("col"),
        ),
        out_specs=P(None, "col", None, None),
        check_vma=False,
    )
```

```python
import functools

import jax
import jax.numpy as jnp
from jax import lax
from jax.experimental import pallas as pl
from jax.experimental.pallas import tpu as pltpu
from jax.sharding import PartitionSpec as P

BITS = {"y": 0, "z0": 1, "z1": 2}
ORDERS = ((("y", "z0", "z1", "z0", "y"), ("z0", "y", "z1", "z0", "y")), (("y", "z1", "z0", "y", "z1"), ("z1", "y", "z0", "z1", "y")), (("y", "z0", "z1", "y", "z0"), ("z0", "y", "z1", "y", "z0")), (("z1", "y", "z0", "z1", "y"), ("y", "z0", "z1", "y", "z0")))
STEPS = (0, 1, 2, 0, 3, 1, 2, 0, 3, 1, 2, 0, 3, 1, 2, 3)
PLACES = (((0, 0), (1, 0), (2, 0), (3, 0), (0, 1)), ((1, 1), (2, 1), (3, 1)))
GROUP = 3
STEPS_PER_OCTAVE = 128.0
TOP = 32512.0
LEAST = 2.0 ** -110
MIB = 2 ** 20
PARAMS = pltpu.CompilerParams(vmem_limit_bytes=40 * MIB)


def widen(green, norb):
    real_part = green[..., :norb]
    imag_part = green[..., norb:]
    lower = jnp.concatenate([-imag_part, real_part], axis=-1)
    return jnp.concatenate([green, lower], axis=-2)


def encode(read, tiles, ni, out_ref):
    rows = []
    for first in range(0, tiles, GROUP):
        values = read(first)
        most = jnp.max(jnp.max(jnp.abs(values), axis=0), axis=0, keepdims=True)
        index = jnp.ceil(jnp.log2(jnp.maximum(most, LEAST) * (1.0 / TOP)) * STEPS_PER_OCTAVE)
        codes = jnp.round(values * jnp.exp2(index * (-1.0 / STEPS_PER_OCTAVE))[None])
        out_ref[first:first + GROUP] = codes.astype(jnp.int32).astype(jnp.int16)
        rows.append(index)
    rows = rows + [jnp.zeros_like(rows[0])] * (ni - len(rows))
    out_ref[tiles] = jnp.concatenate(rows, axis=0).astype(jnp.int32).astype(jnp.int16)


def decode(in_ref, tiles):
    index = in_ref[tiles].astype(jnp.int32).astype(jnp.float32)
    scales = jnp.exp2(index * (1.0 / STEPS_PER_OCTAVE))
    return [
        in_ref[first:first + GROUP].astype(jnp.int32).astype(jnp.float32) * scales[g:g + 1][None]
        for g, first in enumerate(range(0, tiles, GROUP))
    ]


def pack_left(sigma_ref, keep_ref, left_ref, row):
    _, nt, nb, ni, width = sigma_ref.shape
    half = width // 2
    for t in range(nt):
        for b in range(nb):
            ret = sigma_ref[0, t, b] * keep_ref[t, b]
            less = sigma_ref[1, t, b] * keep_ref[t, b]
            cols = slice(b * width, (b + 1) * width)
            rows = slice(row + t * ni, row + (t + 1) * ni)
            left_ref[rows, cols] = jnp.concatenate([ret[:, :half], less[:, :half]], axis=1)
            rows = slice(row + (nt + t) * ni, row + (nt + t + 1) * ni)
            left_ref[rows, cols] = jnp.concatenate([ret[:, half:], less[:, half:]], axis=1)


def own_bits():
    hist = lax.axis_index("hist")
    bits = {d: lax.shift_right_logical(hist, at) & 1 for d, at in BITS.items()}
    return bits, lax.axis_index("col") & 1


def relative(own, core, orders, bits):
    spots = [[lax.bitwise_xor(own[d], bits[d]) for d in order] for order in orders]
    return [one if one is two else jnp.where(core == 0, one, two) for one, two in zip(*spots)]


def spots_of(orders, nt):
    own, core = own_bits()
    dims = [order[:3] for order in orders]
    return [[relative(own, core, dims, {"y": side, "z0": t % 2, "z1": t // 2}) for t in range(nt)] for side in range(2)]


def add_pair(spots, both, pair, term_ref):
    ni, width = term_ref.shape[-2:]
    half_columns = term_ref.shape[3]
    rows = both.shape[0] // 2
    lane = lax.broadcasted_iota(jnp.int32, (rows, width), 1)
    for at in range(2):
        cut = both[:, at * width:(at + 1) * width]
        turned = pltpu.roll(cut[rows:], width // 2, 1)
        value = cut[:rows] + jnp.where(lane < width // 2, -turned, turned)
        side, c = divmod(2 * pair + at, half_columns)
        for t in range(rows // ni):
            term_ref[tuple(spots[side][t]) + (c,)] = value[t * ni:(t + 1) * ni]


def part_kernel(orders, keep_ref, *refs):
    n = len(orders)
    sigma_refs, (gless_ref, gadv_ref) = refs[:n], refs[n:n + 2]
    outs, (left_ref, term_ref) = refs[-2 * n - 2:-2], refs[-2:]
    nb, ncol, norb, width = gless_ref.shape
    rows = left_ref.shape[0] // n
    for at, sigma_ref in enumerate(sigma_refs):
        pack_left(sigma_ref, keep_ref, left_ref, at * rows)
    spots = [spots_of(order, rows // (2 * term_ref.shape[-2])) for order in orders]
    for pair in range(ncol // 2):
        sides = []
        for c in (2 * pair, 2 * pair + 1):
            parts = []
            for b in range(nb):
                parts += [gless_ref[b, c], gadv_ref[b, c]]
            sides.append(jnp.concatenate(parts, axis=0))
        both = jnp.dot(left_ref[...], jnp.concatenate(sides, axis=1), preferred_element_type=jnp.float32)
        for at in range(n):
            add_pair(spots[at], both[at * rows:(at + 1) * rows], pair, term_ref.at[at])
    for at in range(n):
        kept_ref, out_ref = outs[2 * at:2 * at + 2]
        _, n1, n2, half_columns, ni, _ = term_ref.shape[1:]
        kept_ref[0] = term_ref[at, 0]

        def read(first):
            block, c = divmod(first, half_columns)
            a, b = divmod(block, n2)
            return term_ref[at, 1, a, b, c:c + GROUP]

        encode(read, n1 * n2 * half_columns, ni, out_ref)


def fold_kernel(sum_ref, in_ref, *refs):
    keep_ref, out_ref, term_ref = refs[-3:]
    _, nd, nc, ni, width = keep_ref.shape
    tiles = nd * nc
    came = decode(in_ref, 2 * tiles)
    for g, first in enumerate(range(0, tiles, GROUP)):
        d, c = divmod(first, nc)
        keep_ref[0, d, c:c + GROUP] = sum_ref[0, 0, d, c:c + GROUP] + came[g]
        term_ref[first:first + GROUP] = sum_ref[0, 1, d, c:c + GROUP] + came[g + tiles // GROUP]
    encode(lambda first: term_ref[first:first + GROUP], tiles, ni, out_ref)


def cross_kernel(sum_ref, in_ref, *refs):
    out_ref, term_ref = refs[-2:]
    _, nd, nc, ni, width = sum_ref.shape
    for g, came in enumerate(decode(in_ref, nd * nc)):
        d, c = divmod(g * GROUP, nc)
        term_ref[g * GROUP:(g + 1) * GROUP] = sum_ref[0, d, c:c + GROUP] + came
    encode(lambda first: term_ref[first:first + GROUP], nd * nc, ni, out_ref)


def final_kernel(mine_ref, other_ref, *refs):
    out_ref = refs[-1]
    nd, nc, ni, width = out_ref.shape
    mine, other = decode(mine_ref, nd * nc), decode(other_ref, nd * nc)
    half = len(mine) // 2
    for g in range(len(mine)):
        d, c = divmod(g * GROUP, nc)
        out_ref[d, c:c + GROUP] = (mine[g] + other[(g + half) % len(mine)]).astype(jnp.bfloat16)


def merge_kernel(mine_ref, other_ref, *refs):
    out_ref = refs[-1]
    out_ref[0] = mine_ref[...]
    out_ref[1] = other_ref[...]


def copy_kernel(in_ref, *refs):
    refs[-1][...] = in_ref[...]


def place_kernel(items, *refs):
    blocks, out_ref, sem = refs[:len(items)], refs[-2], refs[-1]
    own, core = own_bits()
    copies = []
    for block, (chunk, orders, last) in zip(blocks, items):
        nc, ni, _ = block.shape[-3:]
        row = pl.multiple_of(lax.bitwise_xor(lax.axis_index("col"), chunk) * ni, ni)
        for second in range(2):
            for first in range(2):
                places = []
                for order in orders:
                    bits = dict(zip(order[2:], (first, second, last)))
                    places.append([lax.bitwise_xor(own[d], bits[d]) for d in ("y", "z0", "z1")])
                y, z0, z1 = (jnp.where(core == 0, *pair) for pair in zip(*places))
                target = out_ref.at[2 * z1 + z0, pl.ds(y * nc, nc), pl.ds(row, ni)]
                copies.append(pltpu.make_async_copy(block.at[second, first], target, sem.at[len(copies)]))
    for copy in copies:
        copy.start()
    for copy in copies:
        copy.wait()


def staged(sigma_ret, sigma_less, green_less, green_adv, time_now, col_start, n_hist, n_col):
    nt, nb, ni, width = sigma_ret.shape
    _, ncol, norb, _ = green_less.shape
    nc = ncol // 2
    hist = lax.axis_index("hist")
    def swap(v, chunk, stage):
        pairs = []
        for h in range(n_hist):
            for c in range(n_col):
                partner = h ^ (1 << BITS[ORDERS[chunk][c % 2][stage]])
                pairs.append((h * n_col + c, partner * n_col + c))
        return lax.ppermute(v, ("hist", "col"), pairs)

    def swap_col(v, k):
        return lax.ppermute(v, "col", [(i, i ^ k) for i in range(n_col)])

    vmem = pl.BlockSpec(memory_space=pltpu.VMEM)
    hbm = pl.BlockSpec(memory_space=pltpu.HBM)

    def codes_of(n):
        return jax.ShapeDtypeStruct((n * nc + 1, ni, width), jnp.int16)

    own_sigma = jnp.stack([sigma_ret, sigma_less])
    tbar = hist * nb + jnp.arange(nb, dtype=jnp.int32)
    after = (tbar[:, None] >= col_start[None, :])[:, :, None, None]
    zero = jnp.zeros((), green_less.dtype)
    before = (tbar[None, :] <= time_now[:, None]).astype(sigma_ret.dtype)
    keep = jnp.broadcast_to(before[:, :, None, None], sigma_ret.shape)
    masked = [jnp.where(after, green, zero) for green in (green_less, green_adv)]
    near = swap_col(own_sigma, 1)
    far = swap_col(own_sigma, 2)

    def call(kernel, out_shape, args, before, scratch=(), cost=None):
        args = list(args) + ([] if before is None else [before])
        many = isinstance(out_shape, list)
        return pl.pallas_call(
            kernel,
            out_shape=out_shape,
            in_specs=[vmem] * len(args),
            out_specs=[vmem] * len(out_shape) if many else vmem,
            scratch_shapes=list(scratch),
            compiler_params=PARAMS,
            cost_estimate=cost,
            name=kernel.func.__name__ if isinstance(kernel, functools.partial) else kernel.__name__,
        )(*args)

    def partial(orders, blocks, before):
        n = len(orders)
        rows = 2 * nt * ni
        kept = jax.ShapeDtypeStruct((1, 2, 2, nc, ni, width), jnp.float32)
        flops = 2 * n * rows * 2 * nb * norb * ncol * width
        out = call(
            functools.partial(part_kernel, orders),
            [kept, codes_of(4)] * n,
            [keep, *blocks, *masked],
            before,
            [pltpu.VMEM((n * rows, nb * width), jnp.bfloat16),
             pltpu.VMEM((n, 2, 2, 2, nc, ni, width), jnp.float32)],
            pl.CostEstimate(flops=flops, bytes_accessed=green_less.size * 4, transcendentals=0),
        )
        return [out[2 * at:2 * at + 2] for at in range(n)]

    def terms(n):
        return [pltpu.VMEM((n * nc, ni, width), jnp.float32)]

    def fold(state, chunk, before):
        sums, codes = state
        keep = jax.ShapeDtypeStruct((1, 2, nc, ni, width), jnp.float32)
        state = call(fold_kernel, [keep, codes_of(2)], [sums, swap(codes, chunk, 0)], before, terms(2))
        return state, state[1]

    def cross(state, chunk, before):
        sums, codes = state
        codes = call(cross_kernel, codes_of(2), [sums, swap(codes, chunk, 1)], before, terms(2))
        return codes, codes

    def final(codes, chunk, before):
        out = jax.ShapeDtypeStruct((2, nc, ni, width), jnp.bfloat16)
        out = call(final_kernel, out, [codes, swap(codes, chunk, 2)], before)
        return out, out

    def merge(mine, chunk, before):
        out = jax.ShapeDtypeStruct((2,) + mine.shape, mine.dtype)
        out = call(merge_kernel, out, [mine, swap(mine, chunk, 3)], before)
        return out, out

    def put(items, out):
        extra = [] if out is None else [out]
        n = len(items)
        return pl.pallas_call(
            functools.partial(place_kernel, [(k, ORDERS[k], last) for k, last in items]),
            out_shape=jax.ShapeDtypeStruct((nt, ncol, norb, width), jnp.bfloat16),
            in_specs=[vmem] * n + [hbm] * len(extra),
            out_specs=hbm,
            scratch_shapes=[pltpu.SemaphoreType.DMA((4 * n,))],
            input_output_aliases={n: 0} if extra else {},
            compiler_params=PARAMS,
            name="place_part",
        )(*[blocks[k][last] for k, last in items], *extra)

    state = partial(ORDERS[:2], [own_sigma, near], None)
    passed = call(copy_kernel, jax.ShapeDtypeStruct(far.shape, far.dtype), [far], state[1][1])
    state += partial(ORDERS[2:3], [far], passed)
    state += partial(ORDERS[3:], [swap_col(passed, 1)], state[2][1])
    last = state[3][1]
    todo = [[fold, cross, final, merge] for _ in range(n_col)]
    for k in STEPS:
        state[k], last = todo[k].pop(0)(state[k], k, last)
    blocks = [(state[k], swap(state[k], k, 4)) for k in range(n_col)]
    out = None
    for items in PLACES:
        out = put(items, out)
    return out


def plain(sigma_ret, sigma_less, green_less, green_adv, time_now, col_start):
    norb = green_less.shape[2]
    tb_local = green_less.shape[0]
    full_ret = lax.all_gather(sigma_ret, "col", axis=2, tiled=True)
    full_less = lax.all_gather(sigma_less, "col", axis=2, tiled=True)
    tbar = lax.axis_index("hist") * tb_local + jnp.arange(tb_local, dtype=jnp.int32)
    zero = jnp.zeros((), green_less.dtype)
    before = (tbar[None, :] <= time_now[:, None])[:, :, None, None]
    full_ret = jnp.where(before, full_ret, zero)
    full_less = jnp.where(before, full_less, zero)
    after = (tbar[:, None] >= col_start[None, :])[:, :, None, None]
    b_less = jnp.where(after, widen(green_less, norb), zero)
    b_adv = jnp.where(after, widen(green_adv, norb), zero)
    term = jnp.einsum("tbik,bckn->tcin", full_ret, b_less, preferred_element_type=jnp.float32)
    term = term + jnp.einsum("tbik,bckn->tcin", full_less, b_adv, preferred_element_type=jnp.float32)
    return lax.psum(term, "hist").astype(jnp.bfloat16)


def solution(mesh):
    n_hist, n_col = mesh.shape["hist"], mesh.shape["col"]

    def on_device(*args):
        nt, ncol = args[0].shape[0], args[2].shape[1]
        if n_hist == 8 and nt == 4 and n_col == 4 and ncol % 4 == 0 and ncol % (2 * GROUP) == 0:
            return staged(*args, n_hist, n_col)
        return plain(*args)

    return jax.shard_map(
        on_device,
        mesh=mesh,
        in_specs=(
            P(None, "hist", "col", None),
            P(None, "hist", "col", None),
            P("hist", "col", None, None),
            P("hist", "col", None, None),
            P(),
            P("col"),
        ),
        out_specs=P(None, "col", None, None),
        check_vma=False,
    )
```

```python
import functools

import jax
import jax.numpy as jnp
from jax import lax
from jax.experimental import pallas as pl
from jax.experimental.pallas import tpu as pltpu
from jax.sharding import PartitionSpec as P

BITS = {"y": 0, "z0": 1, "z1": 2}
ORDERS = ((("y", "z0", "z1", "y", "z0"), ("z0", "y", "z1", "z0", "y")), (("y", "z1", "z0", "y", "z1"), ("z1", "y", "z0", "z1", "y")), (("y", "z0", "z1", "y", "z0"), ("z0", "y", "z1", "z0", "y")), (("z1", "y", "z0", "z1", "y"), ("y", "z0", "z1", "y", "z0")))
STEPS = (0, 1, 2, 0, 3, 1, 2, 0, 3, 1, 2, 0, 3, 1, 2, 3)
PLACES = (((0, 0), (1, 0), (2, 0), (3, 0), (0, 1)), ((1, 1), (2, 1), (3, 1)))
GROUP = 3
STEPS_PER_OCTAVE = 128.0
TOP = 32512.0
LEAST = 2.0 ** -110
MIB = 2 ** 20
PARAMS = pltpu.CompilerParams(vmem_limit_bytes=40 * MIB)


def widen(green, norb):
    real_part = green[..., :norb]
    imag_part = green[..., norb:]
    lower = jnp.concatenate([-imag_part, real_part], axis=-1)
    return jnp.concatenate([green, lower], axis=-2)


def encode(read, tiles, ni, out_ref):
    rows = []
    for first in range(0, tiles, GROUP):
        values = read(first)
        most = jnp.max(jnp.max(jnp.abs(values), axis=0), axis=0, keepdims=True)
        index = jnp.ceil(jnp.log2(jnp.maximum(most, LEAST) * (1.0 / TOP)) * STEPS_PER_OCTAVE)
        codes = jnp.round(values * jnp.exp2(index * (-1.0 / STEPS_PER_OCTAVE))[None])
        out_ref[first:first + GROUP] = codes.astype(jnp.int32).astype(jnp.int16)
        rows.append(index)
    rows = rows + [jnp.zeros_like(rows[0])] * (ni - len(rows))
    out_ref[tiles] = jnp.concatenate(rows, axis=0).astype(jnp.int32).astype(jnp.int16)


def decode(in_ref, tiles):
    index = in_ref[tiles].astype(jnp.int32).astype(jnp.float32)
    scales = jnp.exp2(index * (1.0 / STEPS_PER_OCTAVE))
    return [
        in_ref[first:first + GROUP].astype(jnp.int32).astype(jnp.float32) * scales[g:g + 1][None]
        for g, first in enumerate(range(0, tiles, GROUP))
    ]


def pack_left(sigma_ref, keep_ref, left_ref, row):
    _, nt, nb, ni, width = sigma_ref.shape
    half = width // 2
    for t in range(nt):
        for b in range(nb):
            ret = sigma_ref[0, t, b] * keep_ref[t, b]
            less = sigma_ref[1, t, b] * keep_ref[t, b]
            cols = slice(b * width, (b + 1) * width)
            rows = slice(row + t * ni, row + (t + 1) * ni)
            left_ref[rows, cols] = jnp.concatenate([ret[:, :half], less[:, :half]], axis=1)
            rows = slice(row + (nt + t) * ni, row + (nt + t + 1) * ni)
            left_ref[rows, cols] = jnp.concatenate([ret[:, half:], less[:, half:]], axis=1)


def own_bits():
    hist = lax.axis_index("hist")
    bits = {d: lax.shift_right_logical(hist, at) & 1 for d, at in BITS.items()}
    return bits, lax.axis_index("col") & 1


def relative(own, core, orders, bits):
    spots = [[lax.bitwise_xor(own[d], bits[d]) for d in order] for order in orders]
    return [one if one is two else jnp.where(core == 0, one, two) for one, two in zip(*spots)]


def spots_of(orders, nt):
    own, core = own_bits()
    dims = [order[:3] for order in orders]
    return [[relative(own, core, dims, {"y": side, "z0": t % 2, "z1": t // 2}) for t in range(nt)] for side in range(2)]


def add_pair(spots, both, pair, term_ref):
    ni, width = term_ref.shape[-2:]
    half_columns = term_ref.shape[3]
    rows = both.shape[0] // 2
    lane = lax.broadcasted_iota(jnp.int32, (rows, width), 1)
    for at in range(2):
        cut = both[:, at * width:(at + 1) * width]
        turned = pltpu.roll(cut[rows:], width // 2, 1)
        value = cut[:rows] + jnp.where(lane < width // 2, -turned, turned)
        side, c = divmod(2 * pair + at, half_columns)
        for t in range(rows // ni):
            term_ref[tuple(spots[side][t]) + (c,)] = value[t * ni:(t + 1) * ni]


def part_kernel(orders, keep_ref, *refs):
    n = len(orders)
    sigma_refs, (gless_ref, gadv_ref) = refs[:n], refs[n:n + 2]
    outs, (left_ref, term_ref) = refs[-2 * n - 2:-2], refs[-2:]
    nb, ncol, norb, width = gless_ref.shape
    rows = left_ref.shape[0] // n
    for at, sigma_ref in enumerate(sigma_refs):
        pack_left(sigma_ref, keep_ref, left_ref, at * rows)
    spots = [spots_of(order, rows // (2 * term_ref.shape[-2])) for order in orders]
    for pair in range(ncol // 2):
        sides = []
        for c in (2 * pair, 2 * pair + 1):
            parts = []
            for b in range(nb):
                parts += [gless_ref[b, c], gadv_ref[b, c]]
            sides.append(jnp.concatenate(parts, axis=0))
        both = jnp.dot(left_ref[...], jnp.concatenate(sides, axis=1), preferred_element_type=jnp.float32)
        for at in range(n):
            add_pair(spots[at], both[at * rows:(at + 1) * rows], pair, term_ref.at[at])
    for at in range(n):
        kept_ref, out_ref = outs[2 * at:2 * at + 2]
        _, n1, n2, half_columns, ni, _ = term_ref.shape[1:]
        kept_ref[0] = term_ref[at, 0]

        def read(first):
            block, c = divmod(first, half_columns)
            a, b = divmod(block, n2)
            return term_ref[at, 1, a, b, c:c + GROUP]

        encode(read, n1 * n2 * half_columns, ni, out_ref)


def fold_kernel(sum_ref, in_ref, *refs):
    keep_ref, out_ref, term_ref = refs[-3:]
    _, nd, nc, ni, width = keep_ref.shape
    tiles = nd * nc
    came = decode(in_ref, 2 * tiles)
    for g, first in enumerate(range(0, tiles, GROUP)):
        d, c = divmod(first, nc)
        keep_ref[0, d, c:c + GROUP] = sum_ref[0, 0, d, c:c + GROUP] + came[g]
        term_ref[first:first + GROUP] = sum_ref[0, 1, d, c:c + GROUP] + came[g + tiles // GROUP]
    encode(lambda first: term_ref[first:first + GROUP], tiles, ni, out_ref)


def cross_kernel(sum_ref, in_ref, *refs):
    out_ref, term_ref = refs[-2:]
    _, nd, nc, ni, width = sum_ref.shape
    for g, came in enumerate(decode(in_ref, nd * nc)):
        d, c = divmod(g * GROUP, nc)
        term_ref[g * GROUP:(g + 1) * GROUP] = sum_ref[0, d, c:c + GROUP] + came
    encode(lambda first: term_ref[first:first + GROUP], nd * nc, ni, out_ref)


def final_kernel(mine_ref, other_ref, *refs):
    out_ref = refs[-1]
    nd, nc, ni, width = out_ref.shape
    mine, other = decode(mine_ref, nd * nc), decode(other_ref, nd * nc)
    half = len(mine) // 2
    for g in range(len(mine)):
        d, c = divmod(g * GROUP, nc)
        out_ref[d, c:c + GROUP] = (mine[g] + other[(g + half) % len(mine)]).astype(jnp.bfloat16)


def merge_kernel(mine_ref, other_ref, *refs):
    out_ref = refs[-1]
    out_ref[0] = mine_ref[...]
    out_ref[1] = other_ref[...]


def copy_kernel(in_ref, *refs):
    refs[-1][...] = in_ref[...]


def place_kernel(items, *refs):
    blocks, out_ref, sem = refs[:len(items)], refs[-2], refs[-1]
    own, core = own_bits()
    copies = []
    for block, (chunk, orders, last) in zip(blocks, items):
        nc, ni, _ = block.shape[-3:]
        row = pl.multiple_of(lax.bitwise_xor(lax.axis_index("col"), chunk) * ni, ni)
        for second in range(2):
            for first in range(2):
                places = []
                for order in orders:
                    bits = dict(zip(order[2:], (first, second, last)))
                    places.append([lax.bitwise_xor(own[d], bits[d]) for d in ("y", "z0", "z1")])
                y, z0, z1 = (jnp.where(core == 0, *pair) for pair in zip(*places))
                target = out_ref.at[2 * z1 + z0, pl.ds(y * nc, nc), pl.ds(row, ni)]
                copies.append(pltpu.make_async_copy(block.at[second, first], target, sem.at[len(copies)]))
    for copy in copies:
        copy.start()
    for copy in copies:
        copy.wait()


def staged(sigma_ret, sigma_less, green_less, green_adv, time_now, col_start, n_hist, n_col):
    nt, nb, ni, width = sigma_ret.shape
    _, ncol, norb, _ = green_less.shape
    nc = ncol // 2
    hist = lax.axis_index("hist")
    def swap(v, chunk, stage):
        pairs = []
        for h in range(n_hist):
            for c in range(n_col):
                partner = h ^ (1 << BITS[ORDERS[chunk][c % 2][stage]])
                pairs.append((h * n_col + c, partner * n_col + c))
        return lax.ppermute(v, ("hist", "col"), pairs)

    def swap_col(v, k):
        return lax.ppermute(v, "col", [(i, i ^ k) for i in range(n_col)])

    vmem = pl.BlockSpec(memory_space=pltpu.VMEM)
    hbm = pl.BlockSpec(memory_space=pltpu.HBM)

    def codes_of(n):
        return jax.ShapeDtypeStruct((n * nc + 1, ni, width), jnp.int16)

    own_sigma = jnp.stack([sigma_ret, sigma_less])
    tbar = hist * nb + jnp.arange(nb, dtype=jnp.int32)
    after = (tbar[:, None] >= col_start[None, :])[:, :, None, None]
    zero = jnp.zeros((), green_less.dtype)
    before = (tbar[None, :] <= time_now[:, None]).astype(sigma_ret.dtype)
    keep = jnp.broadcast_to(before[:, :, None, None], sigma_ret.shape)
    masked = [jnp.where(after, green, zero) for green in (green_less, green_adv)]
    near = swap_col(own_sigma, 1)
    far = swap_col(own_sigma, 2)

    def call(kernel, out_shape, args, before, scratch=(), cost=None):
        args = list(args) + ([] if before is None else [before])
        many = isinstance(out_shape, list)
        return pl.pallas_call(
            kernel,
            out_shape=out_shape,
            in_specs=[vmem] * len(args),
            out_specs=[vmem] * len(out_shape) if many else vmem,
            scratch_shapes=list(scratch),
            compiler_params=PARAMS,
            cost_estimate=cost,
            name=kernel.func.__name__ if isinstance(kernel, functools.partial) else kernel.__name__,
        )(*args)

    def partial(orders, blocks, before):
        n = len(orders)
        rows = 2 * nt * ni
        kept = jax.ShapeDtypeStruct((1, 2, 2, nc, ni, width), jnp.float32)
        flops = 2 * n * rows * 2 * nb * norb * ncol * width
        out = call(
            functools.partial(part_kernel, orders),
            [kept, codes_of(4)] * n,
            [keep, *blocks, *masked],
            before,
            [pltpu.VMEM((n * rows, nb * width), jnp.bfloat16),
             pltpu.VMEM((n, 2, 2, 2, nc, ni, width), jnp.float32)],
            pl.CostEstimate(flops=flops, bytes_accessed=green_less.size * 4, transcendentals=0),
        )
        return [out[2 * at:2 * at + 2] for at in range(n)]

    def terms(n):
        return [pltpu.VMEM((n * nc, ni, width), jnp.float32)]

    def fold(state, chunk, before):
        sums, codes = state
        keep = jax.ShapeDtypeStruct((1, 2, nc, ni, width), jnp.float32)
        state = call(fold_kernel, [keep, codes_of(2)], [sums, swap(codes, chunk, 0)], before, terms(2))
        return state, state[1]

    def cross(state, chunk, before):
        sums, codes = state
        codes = call(cross_kernel, codes_of(2), [sums, swap(codes, chunk, 1)], before, terms(2))
        return codes, codes

    def final(codes, chunk, before):
        out = jax.ShapeDtypeStruct((2, nc, ni, width), jnp.bfloat16)
        out = call(final_kernel, out, [codes, swap(codes, chunk, 2)], before)
        return out, out

    def merge(mine, chunk, before):
        out = jax.ShapeDtypeStruct((2,) + mine.shape, mine.dtype)
        out = call(merge_kernel, out, [mine, swap(mine, chunk, 3)], before)
        return out, out

    def put(items, out):
        extra = [] if out is None else [out]
        n = len(items)
        return pl.pallas_call(
            functools.partial(place_kernel, [(k, ORDERS[k], last) for k, last in items]),
            out_shape=jax.ShapeDtypeStruct((nt, ncol, norb, width), jnp.bfloat16),
            in_specs=[vmem] * n + [hbm] * len(extra),
            out_specs=hbm,
            scratch_shapes=[pltpu.SemaphoreType.DMA((4 * n,))],
            input_output_aliases={n: 0} if extra else {},
            compiler_params=PARAMS,
            name="place_part",
        )(*[blocks[k][last] for k, last in items], *extra)

    state = partial(ORDERS[:2], [own_sigma, near], None)
    passed = call(copy_kernel, jax.ShapeDtypeStruct(far.shape, far.dtype), [far], state[1][1])
    state += partial(ORDERS[2:3], [far], passed)
    state += partial(ORDERS[3:], [swap_col(passed, 1)], state[2][1])
    last = state[3][1]
    todo = [[fold, cross, final, merge] for _ in range(n_col)]
    for k in STEPS:
        state[k], last = todo[k].pop(0)(state[k], k, last)
    blocks = [(state[k], swap(state[k], k, 4)) for k in range(n_col)]
    out = None
    for items in PLACES:
        out = put(items, out)
    return out


def plain(sigma_ret, sigma_less, green_less, green_adv, time_now, col_start):
    norb = green_less.shape[2]
    tb_local = green_less.shape[0]
    full_ret = lax.all_gather(sigma_ret, "col", axis=2, tiled=True)
    full_less = lax.all_gather(sigma_less, "col", axis=2, tiled=True)
    tbar = lax.axis_index("hist") * tb_local + jnp.arange(tb_local, dtype=jnp.int32)
    zero = jnp.zeros((), green_less.dtype)
    before = (tbar[None, :] <= time_now[:, None])[:, :, None, None]
    full_ret = jnp.where(before, full_ret, zero)
    full_less = jnp.where(before, full_less, zero)
    after = (tbar[:, None] >= col_start[None, :])[:, :, None, None]
    b_less = jnp.where(after, widen(green_less, norb), zero)
    b_adv = jnp.where(after, widen(green_adv, norb), zero)
    term = jnp.einsum("tbik,bckn->tcin", full_ret, b_less, preferred_element_type=jnp.float32)
    term = term + jnp.einsum("tbik,bckn->tcin", full_less, b_adv, preferred_element_type=jnp.float32)
    return lax.psum(term, "hist").astype(jnp.bfloat16)


def solution(mesh):
    n_hist, n_col = mesh.shape["hist"], mesh.shape["col"]

    def on_device(*args):
        nt, ncol = args[0].shape[0], args[2].shape[1]
        if n_hist == 8 and nt == 4 and n_col == 4 and ncol % 4 == 0 and ncol % (2 * GROUP) == 0:
            return staged(*args, n_hist, n_col)
        return plain(*args)

    return jax.shard_map(
        on_device,
        mesh=mesh,
        in_specs=(
            P(None, "hist", "col", None),
            P(None, "hist", "col", None),
            P("hist", "col", None, None),
            P("hist", "col", None, None),
            P(),
            P("col"),
        ),
        out_specs=P(None, "col", None, None),
        check_vma=False,
    )
```

```python
import functools

import jax
import jax.numpy as jnp
from jax import lax
from jax.experimental import pallas as pl
from jax.experimental.pallas import tpu as pltpu
from jax.sharding import PartitionSpec as P

BITS = {"y": 0, "z0": 1, "z1": 2}
ORDERS = ((("y", "z0", "z1", "z0", "y"), ("z0", "y", "z1", "z0", "y")), (("y", "z1", "z0", "y", "z1"), ("z1", "y", "z0", "z1", "y")), (("y", "z0", "z1", "y", "z0"), ("z0", "y", "z1", "z0", "y")), (("z1", "y", "z0", "z1", "y"), ("y", "z0", "z1", "y", "z0")))
STEPS = (0, 1, 2, 0, 3, 1, 2, 3, 0, 1, 2, 3, 0, 1, 2, 3)
PLACES = (((0, 0), (1, 0), (2, 0), (3, 0), (0, 1)), ((1, 1), (2, 1), (3, 1)))
GROUP = 3
STEPS_PER_OCTAVE = 128.0
TOP = 32512.0
LEAST = 2.0 ** -110
MIB = 2 ** 20
PARAMS = pltpu.CompilerParams(vmem_limit_bytes=40 * MIB)


def widen(green, norb):
    real_part = green[..., :norb]
    imag_part = green[..., norb:]
    lower = jnp.concatenate([-imag_part, real_part], axis=-1)
    return jnp.concatenate([green, lower], axis=-2)


def encode(read, tiles, ni, out_ref):
    rows = []
    for first in range(0, tiles, GROUP):
        values = read(first)
        most = jnp.max(jnp.max(jnp.abs(values), axis=0), axis=0, keepdims=True)
        index = jnp.ceil(jnp.log2(jnp.maximum(most, LEAST) * (1.0 / TOP)) * STEPS_PER_OCTAVE)
        codes = jnp.round(values * jnp.exp2(index * (-1.0 / STEPS_PER_OCTAVE))[None])
        out_ref[first:first + GROUP] = codes.astype(jnp.int32).astype(jnp.int16)
        rows.append(index)
    rows = rows + [jnp.zeros_like(rows[0])] * (ni - len(rows))
    out_ref[tiles] = jnp.concatenate(rows, axis=0).astype(jnp.int32).astype(jnp.int16)


def decode(in_ref, tiles):
    index = in_ref[tiles].astype(jnp.int32).astype(jnp.float32)
    scales = jnp.exp2(index * (1.0 / STEPS_PER_OCTAVE))
    return [
        in_ref[first:first + GROUP].astype(jnp.int32).astype(jnp.float32) * scales[g:g + 1][None]
        for g, first in enumerate(range(0, tiles, GROUP))
    ]


def pack_left(sigma_ref, keep_ref, left_ref, row):
    _, nt, nb, ni, width = sigma_ref.shape
    half = width // 2
    for t in range(nt):
        for b in range(nb):
            ret = sigma_ref[0, t, b] * keep_ref[t, b]
            less = sigma_ref[1, t, b] * keep_ref[t, b]
            cols = slice(b * width, (b + 1) * width)
            rows = slice(row + t * ni, row + (t + 1) * ni)
            left_ref[rows, cols] = jnp.concatenate([ret[:, :half], less[:, :half]], axis=1)
            rows = slice(row + (nt + t) * ni, row + (nt + t + 1) * ni)
            left_ref[rows, cols] = jnp.concatenate([ret[:, half:], less[:, half:]], axis=1)


def own_bits():
    hist = lax.axis_index("hist")
    bits = {d: lax.shift_right_logical(hist, at) & 1 for d, at in BITS.items()}
    return bits, lax.axis_index("col") & 1


def relative(own, core, orders, bits):
    spots = [[lax.bitwise_xor(own[d], bits[d]) for d in order] for order in orders]
    return [one if one is two else jnp.where(core == 0, one, two) for one, two in zip(*spots)]


def spots_of(orders, nt):
    own, core = own_bits()
    dims = [order[:3] for order in orders]
    return [[relative(own, core, dims, {"y": side, "z0": t % 2, "z1": t // 2}) for t in range(nt)] for side in range(2)]


def add_pair(spots, both, pair, term_ref):
    ni, width = term_ref.shape[-2:]
    half_columns = term_ref.shape[3]
    rows = both.shape[0] // 2
    lane = lax.broadcasted_iota(jnp.int32, (rows, width), 1)
    for at in range(2):
        cut = both[:, at * width:(at + 1) * width]
        turned = pltpu.roll(cut[rows:], width // 2, 1)
        value = cut[:rows] + jnp.where(lane < width // 2, -turned, turned)
        side, c = divmod(2 * pair + at, half_columns)
        for t in range(rows // ni):
            term_ref[tuple(spots[side][t]) + (c,)] = value[t * ni:(t + 1) * ni]


def part_kernel(orders, keep_ref, *refs):
    n = len(orders)
    sigma_refs, (gless_ref, gadv_ref) = refs[:n], refs[n:n + 2]
    outs, (left_ref, term_ref) = refs[-2 * n - 2:-2], refs[-2:]
    nb, ncol, norb, width = gless_ref.shape
    rows = left_ref.shape[0] // n
    for at, sigma_ref in enumerate(sigma_refs):
        pack_left(sigma_ref, keep_ref, left_ref, at * rows)
    spots = [spots_of(order, rows // (2 * term_ref.shape[-2])) for order in orders]
    for pair in range(ncol // 2):
        sides = []
        for c in (2 * pair, 2 * pair + 1):
            parts = []
            for b in range(nb):
                parts += [gless_ref[b, c], gadv_ref[b, c]]
            sides.append(jnp.concatenate(parts, axis=0))
        both = jnp.dot(left_ref[...], jnp.concatenate(sides, axis=1), preferred_element_type=jnp.float32)
        for at in range(n):
            add_pair(spots[at], both[at * rows:(at + 1) * rows], pair, term_ref.at[at])
    for at in range(n):
        kept_ref, out_ref = outs[2 * at:2 * at + 2]
        _, n1, n2, half_columns, ni, _ = term_ref.shape[1:]
        kept_ref[0] = term_ref[at, 0]

        def read(first):
            block, c = divmod(first, half_columns)
            a, b = divmod(block, n2)
            return term_ref[at, 1, a, b, c:c + GROUP]

        encode(read, n1 * n2 * half_columns, ni, out_ref)


def fold_kernel(sum_ref, in_ref, *refs):
    keep_ref, out_ref, term_ref = refs[-3:]
    _, nd, nc, ni, width = keep_ref.shape
    tiles = nd * nc
    came = decode(in_ref, 2 * tiles)
    for g, first in enumerate(range(0, tiles, GROUP)):
        d, c = divmod(first, nc)
        keep_ref[0, d, c:c + GROUP] = sum_ref[0, 0, d, c:c + GROUP] + came[g]
        term_ref[first:first + GROUP] = sum_ref[0, 1, d, c:c + GROUP] + came[g + tiles // GROUP]
    encode(lambda first: term_ref[first:first + GROUP], tiles, ni, out_ref)


def cross_kernel(sum_ref, in_ref, *refs):
    out_ref, term_ref = refs[-2:]
    _, nd, nc, ni, width = sum_ref.shape
    for g, came in enumerate(decode(in_ref, nd * nc)):
        d, c = divmod(g * GROUP, nc)
        term_ref[g * GROUP:(g + 1) * GROUP] = sum_ref[0, d, c:c + GROUP] + came
    encode(lambda first: term_ref[first:first + GROUP], nd * nc, ni, out_ref)


def final_kernel(mine_ref, other_ref, *refs):
    out_ref = refs[-1]
    nd, nc, ni, width = out_ref.shape
    mine, other = decode(mine_ref, nd * nc), decode(other_ref, nd * nc)
    half = len(mine) // 2
    for g in range(len(mine)):
        d, c = divmod(g * GROUP, nc)
        out_ref[d, c:c + GROUP] = (mine[g] + other[(g + half) % len(mine)]).astype(jnp.bfloat16)


def merge_kernel(mine_ref, other_ref, *refs):
    out_ref = refs[-1]
    out_ref[0] = mine_ref[...]
    out_ref[1] = other_ref[...]


def copy_kernel(in_ref, *refs):
    refs[-1][...] = in_ref[...]


def place_kernel(items, *refs):
    blocks, out_ref, sem = refs[:len(items)], refs[-2], refs[-1]
    own, core = own_bits()
    copies = []
    for block, (chunk, orders, last) in zip(blocks, items):
        nc, ni, _ = block.shape[-3:]
        row = pl.multiple_of(lax.bitwise_xor(lax.axis_index("col"), chunk) * ni, ni)
        for second in range(2):
            for first in range(2):
                places = []
                for order in orders:
                    bits = dict(zip(order[2:], (first, second, last)))
                    places.append([lax.bitwise_xor(own[d], bits[d]) for d in ("y", "z0", "z1")])
                y, z0, z1 = (jnp.where(core == 0, *pair) for pair in zip(*places))
                target = out_ref.at[2 * z1 + z0, pl.ds(y * nc, nc), pl.ds(row, ni)]
                copies.append(pltpu.make_async_copy(block.at[second, first], target, sem.at[len(copies)]))
    for copy in copies:
        copy.start()
    for copy in copies:
        copy.wait()


def staged(sigma_ret, sigma_less, green_less, green_adv, time_now, col_start, n_hist, n_col):
    nt, nb, ni, width = sigma_ret.shape
    _, ncol, norb, _ = green_less.shape
    nc = ncol // 2
    hist = lax.axis_index("hist")
    def swap(v, chunk, stage):
        pairs = []
        for h in range(n_hist):
            for c in range(n_col):
                partner = h ^ (1 << BITS[ORDERS[chunk][c % 2][stage]])
                pairs.append((h * n_col + c, partner * n_col + c))
        return lax.ppermute(v, ("hist", "col"), pairs)

    def swap_col(v, k):
        return lax.ppermute(v, "col", [(i, i ^ k) for i in range(n_col)])

    vmem = pl.BlockSpec(memory_space=pltpu.VMEM)
    hbm = pl.BlockSpec(memory_space=pltpu.HBM)

    def codes_of(n):
        return jax.ShapeDtypeStruct((n * nc + 1, ni, width), jnp.int16)

    own_sigma = jnp.stack([sigma_ret, sigma_less])
    tbar = hist * nb + jnp.arange(nb, dtype=jnp.int32)
    after = (tbar[:, None] >= col_start[None, :])[:, :, None, None]
    zero = jnp.zeros((), green_less.dtype)
    before = (tbar[None, :] <= time_now[:, None]).astype(sigma_ret.dtype)
    keep = jnp.broadcast_to(before[:, :, None, None], sigma_ret.shape)
    masked = [jnp.where(after, green, zero) for green in (green_less, green_adv)]
    near = swap_col(own_sigma, 1)
    far = swap_col(own_sigma, 2)

    def call(kernel, out_shape, args, before, scratch=(), cost=None):
        args = list(args) + ([] if before is None else [before])
        many = isinstance(out_shape, list)
        return pl.pallas_call(
            kernel,
            out_shape=out_shape,
            in_specs=[vmem] * len(args),
            out_specs=[vmem] * len(out_shape) if many else vmem,
            scratch_shapes=list(scratch),
            compiler_params=PARAMS,
            cost_estimate=cost,
            name=kernel.func.__name__ if isinstance(kernel, functools.partial) else kernel.__name__,
        )(*args)

    def partial(orders, blocks, before):
        n = len(orders)
        rows = 2 * nt * ni
        kept = jax.ShapeDtypeStruct((1, 2, 2, nc, ni, width), jnp.float32)
        flops = 2 * n * rows * 2 * nb * norb * ncol * width
        out = call(
            functools.partial(part_kernel, orders),
            [kept, codes_of(4)] * n,
            [keep, *blocks, *masked],
            before,
            [pltpu.VMEM((n * rows, nb * width), jnp.bfloat16),
             pltpu.VMEM((n, 2, 2, 2, nc, ni, width), jnp.float32)],
            pl.CostEstimate(flops=flops, bytes_accessed=green_less.size * 4, transcendentals=0),
        )
        return [out[2 * at:2 * at + 2] for at in range(n)]

    def terms(n):
        return [pltpu.VMEM((n * nc, ni, width), jnp.float32)]

    def fold(state, chunk, before):
        sums, codes = state
        keep = jax.ShapeDtypeStruct((1, 2, nc, ni, width), jnp.float32)
        state = call(fold_kernel, [keep, codes_of(2)], [sums, swap(codes, chunk, 0)], before, terms(2))
        return state, state[1]

    def cross(state, chunk, before):
        sums, codes = state
        codes = call(cross_kernel, codes_of(2), [sums, swap(codes, chunk, 1)], before, terms(2))
        return codes, codes

    def final(codes, chunk, before):
        out = jax.ShapeDtypeStruct((2, nc, ni, width), jnp.bfloat16)
        out = call(final_kernel, out, [codes, swap(codes, chunk, 2)], before)
        return out, out

    def merge(mine, chunk, before):
        out = jax.ShapeDtypeStruct((2,) + mine.shape, mine.dtype)
        out = call(merge_kernel, out, [mine, swap(mine, chunk, 3)], before)
        return out, out

    def put(items, out):
        extra = [] if out is None else [out]
        n = len(items)
        return pl.pallas_call(
            functools.partial(place_kernel, [(k, ORDERS[k], last) for k, last in items]),
            out_shape=jax.ShapeDtypeStruct((nt, ncol, norb, width), jnp.bfloat16),
            in_specs=[vmem] * n + [hbm] * len(extra),
            out_specs=hbm,
            scratch_shapes=[pltpu.SemaphoreType.DMA((4 * n,))],
            input_output_aliases={n: 0} if extra else {},
            compiler_params=PARAMS,
            name="place_part",
        )(*[blocks[k][last] for k, last in items], *extra)

    state = partial(ORDERS[:2], [own_sigma, near], None)
    passed = call(copy_kernel, jax.ShapeDtypeStruct(far.shape, far.dtype), [far], state[1][1])
    state += partial(ORDERS[2:3], [far], passed)
    state += partial(ORDERS[3:], [swap_col(passed, 1)], state[2][1])
    last = state[3][1]
    todo = [[fold, cross, final, merge] for _ in range(n_col)]
    for k in STEPS:
        state[k], last = todo[k].pop(0)(state[k], k, last)
    blocks = [(state[k], swap(state[k], k, 4)) for k in range(n_col)]
    out = None
    for items in PLACES:
        out = put(items, out)
    return out


def plain(sigma_ret, sigma_less, green_less, green_adv, time_now, col_start):
    norb = green_less.shape[2]
    tb_local = green_less.shape[0]
    full_ret = lax.all_gather(sigma_ret, "col", axis=2, tiled=True)
    full_less = lax.all_gather(sigma_less, "col", axis=2, tiled=True)
    tbar = lax.axis_index("hist") * tb_local + jnp.arange(tb_local, dtype=jnp.int32)
    zero = jnp.zeros((), green_less.dtype)
    before = (tbar[None, :] <= time_now[:, None])[:, :, None, None]
    full_ret = jnp.where(before, full_ret, zero)
    full_less = jnp.where(before, full_less, zero)
    after = (tbar[:, None] >= col_start[None, :])[:, :, None, None]
    b_less = jnp.where(after, widen(green_less, norb), zero)
    b_adv = jnp.where(after, widen(green_adv, norb), zero)
    term = jnp.einsum("tbik,bckn->tcin", full_ret, b_less, preferred_element_type=jnp.float32)
    term = term + jnp.einsum("tbik,bckn->tcin", full_less, b_adv, preferred_element_type=jnp.float32)
    return lax.psum(term, "hist").astype(jnp.bfloat16)


def solution(mesh):
    n_hist, n_col = mesh.shape["hist"], mesh.shape["col"]

    def on_device(*args):
        nt, ncol = args[0].shape[0], args[2].shape[1]
        if n_hist == 8 and nt == 4 and n_col == 4 and ncol % 4 == 0 and ncol % (2 * GROUP) == 0:
            return staged(*args, n_hist, n_col)
        return plain(*args)

    return jax.shard_map(
        on_device,
        mesh=mesh,
        in_specs=(
            P(None, "hist", "col", None),
            P(None, "hist", "col", None),
            P("hist", "col", None, None),
            P("hist", "col", None, None),
            P(),
            P("col"),
        ),
        out_specs=P(None, "col", None, None),
        check_vma=False,
    )
```
